512 devices in a mesh: seq: 64 (over z, y), mp: 4 (over x), dp: 2 (over core).
Axes of the slice: x: 4, y: 8, z: 8, core: 2. Of those that a mesh axis runs over, the one named last changes fastest.
Arguments:
- enc_tokens: bfloat16 [4, 2048, 1280], P('dp', 'seq'), may hold values from -6 to 6
- enc_gain: float32 [1280], replicated, may hold values from 0.4 to 1.6
- enc_bias: float32 [1280], replicated, may hold values from -3 to 3
- w_in: bfloat16 [1280, 2560], P(None, 'mp'), may hold values from -0.15625 to 0.15625
- w_out: bfloat16 [2560, 1280], P('mp'), may hold values from -0.125 to 0.125
- final_gain: float32 [1280], replicated, may hold values from 0.4 to 1.6
- w_embed: bfloat16 [1280, 512], P(None, 'mp'), may hold values from -0.15625 to 0.15625
- dest: int32 [4, 2048, 1], P('dp', 'seq'), may hold values from 0 to 63; in each aligned block of 32 rows (0 to 31, 32 to 63, ..., all dimensions but the last counted through in order) at most 2 rows name the same one
- mask_token: bfloat16 [512], replicated, may hold values from -4 to 4
- dec_gain: float32 [512], replicated, may hold values from 0.4 to 1.6
- w_query: bfloat16 [512, 256], P(None, 'mp'), may hold values from -10 to 10
- w_key: bfloat16 [512, 256], P(None, 'mp'), may hold values from -0.25 to 0.25
- w_value: bfloat16 [512, 256], P(None, 'mp'), may hold values from -0.25 to 0.25
- w_proj: bfloat16 [256, 512], P('mp'), may hold values from -1 to 1
Outputs:
- decoded: bfloat16 [4, 8192, 512], P('dp', ('seq', 'mp'))
The draws below stay inside these ranges and needn't reach their ends.
Inputs may be any that keep to these rules, and one draw needn't show every extreme that they name: `dest`: in each aligned block of 32 rows of an image (the rows of one index of seq) no tile is named more than 2 times.
All inputs are finite; a program needn't handle non-finite values.
Results may differ from the reference program's by a relative error of at most 0.033.
Values may be sent and summed in bfloat16 or wider, within the bound.
A program may use at most 64 MiB of HBM per device.

```python
import math
import jax
import jax.numpy as jnp
import numpy as np
from jax import lax

DE = 1280
FFW = 2560
DD = 512
HEADS = 8
HD = 32
DH = 256
PATCH_DEV = 128
VIS_DEV = 32
MOST = 2
IMAGES = 4
PATCHES = 8192
VIS = 2048
N_SEQ = 64


def draw_w_query(key, part):
    base = jnp.clip(jax.random.normal(jax.random.fold_in(key, 11), (DD, DH), jnp.float32), -4.0, 4.0) * 0.1
    return base.astype(jnp.bfloat16)


def block_scale(own_key, extent, pieces, least, top_value):
    def one(dim, blocks):
        steps = jax.random.uniform(jax.random.fold_in(jax.random.fold_in(own_key, 6), dim), (blocks,), jnp.float32, least / len(pieces), top_value / len(pieces))
        return jnp.repeat(jnp.exp(steps), extent[dim] // blocks).reshape((-1,) + (1,) * (len(extent) - dim - 1))

    level = one(*pieces[0])
    for cut in pieces[1:]:
        level = level * one(*cut)
    return level


def routed_block(key, own, number, rows, count, top, bound, lean):
    order = jax.random.permutation(key, count)
    crowded, usual = portions_of(count, rows * top, bound, lean, True), portions_of(count, rows * top, bound, lean, False)
    places = jnp.arange(count)

    def named(tallies, turn):
        used = int((tallies > 0).sum())
        fixed = max(1, used // 4)
        passed = fixed + (places - fixed + turn * (used - fixed)) % max(1, count - fixed)
        return jnp.zeros((count,), jnp.int32).at[order[jnp.where(places < fixed, places, passed)]].set(jnp.asarray(tallies, jnp.int32))

    tallies = jnp.where(number % 4 == 0, named(crowded, number // 4), named(usual, number - number // 4 - 1))
    mixed = jax.random.permutation(jax.random.fold_in(own, 3), count)
    donor, taker = mixed[0:count // 2 * 2:2], mixed[1:count // 2 * 2:2]
    margin = jnp.minimum(tallies[donor] - 1, bound - tallies[taker]) // 2
    margin = jnp.where((donor == order[0]) | (taker == order[0]) | (tallies[taker] == 0), 0, jnp.maximum(margin, 0))
    passed = jax.random.randint(jax.random.fold_in(own, 4), (count // 2,), 0, 1 << 20) % (margin + 1)
    tallies = tallies.at[donor].add(-passed).at[taker].add(passed)
    items = jnp.searchsorted(jnp.cumsum(tallies), jnp.arange(rows * top), side="right").astype(jnp.int32)
    listing = items.reshape(top, rows).T
    listing = listing[jax.random.permutation(jax.random.fold_in(own, 1), rows)]
    turn = jax.random.randint(jax.random.fold_in(own, 2), (rows, 1), 0, top)
    return jnp.take_along_axis(listing, (jnp.arange(top)[None, :] + turn) % top, axis=1)


def portions_of(number_of, total, reach, skew, full):
    portions = [(1 << 20) // math.isqrt(standing ** skew) + 1 for standing in range(1, number_of + 1)]
    largest = reach if full else min(reach, max(-(-total // number_of), total * portions[0] // sum(portions)))
    least = 1 if total - largest >= number_of - 1 else 0
    given, spare = [largest] + [least] * (number_of - 1), total - largest - least * (number_of - 1)
    while spare > 0:
        movable = [i for i in range(1, number_of) if given[i] < largest] or [i for i in range(1, number_of) if given[i] < reach]
        whole, remaining = sum([portions[i] for i in movable]), spare
        for i in movable:
            extra = min(reach - given[i], max(1, remaining * portions[i] // whole), spare)
            given[i] = given[i] + extra
            spare = spare - extra
    return np.array(given)


def centred(stream_key, extent, scale, most, pieces=(), kind=jnp.bfloat16):
    entries = scale * jax.random.normal(stream_key, extent, jnp.float32)
    if pieces:
        entries = entries * block_scale(stream_key, extent, pieces, -0.22, 0.18)
    return jnp.clip(entries, -most, most).astype(kind)


def setup_inputs(seed: int = 0) -> dict:
    splits = jax.random.split(jax.random.key(seed), 15)
    enc_tokens = centred(splits[0], (IMAGES, VIS, DE), 1.0, 6.0, ((0, 2), (1, 64)))
    enc_gain = jnp.clip(jax.random.uniform(splits[1], (DE,), jnp.float32, 0.4, 1.6), 0.4, 1.6)
    enc_bias = centred(splits[2], (DE,), 0.5, 3.0, (), jnp.float32)
    w_in = centred(splits[3], (DE, FFW), DE ** -0.5, 0.15625, ((1, 4),))
    w_out = centred(splits[4], (FFW, DE), FFW ** -0.5, 0.125, ((0, 4),))
    final_gain = jnp.clip(jax.random.uniform(splits[5], (DE,), jnp.float32, 0.4, 1.6), 0.4, 1.6)
    w_embed = centred(splits[6], (DE, DD), DE ** -0.5, 0.15625, ((1, 4),))
    dest_keys = jax.random.split(jax.random.fold_in(splits[7], 1), IMAGES * VIS // VIS_DEV)
    dest_turns = jax.random.permutation(jax.random.fold_in(splits[7], 3), IMAGES * VIS // VIS_DEV)
    dest = jax.vmap(lambda own, number: routed_block(jax.random.fold_in(splits[7], 2), own, number, VIS_DEV, N_SEQ, 1, MOST, 2))(dest_keys, dest_turns).reshape((IMAGES, VIS, 1))
    mask_token = centred(splits[8], (DD,), 1.0, 4.0)
    dec_gain = jnp.clip(jax.random.uniform(splits[9], (DD,), jnp.float32, 0.4, 1.6), 0.4, 1.6)
    w_query = draw_w_query(jax.random.fold_in(splits[14], 71), 0)
    w_key = centred(splits[11], (DD, DH), DD ** -0.5, 0.25, ((1, 4),))
    w_value = centred(splits[12], (DD, DH), DD ** -0.5, 0.25, ((1, 4),))
    w_proj = centred(splits[13], (DH, DD), 0.2, 1.0, ((0, 4),))
    return {"enc_tokens": enc_tokens, "enc_gain": enc_gain, "enc_bias": enc_bias, "w_in": w_in, "w_out": w_out, "final_gain": final_gain, "w_embed": w_embed, "dest": dest, "mask_token": mask_token, "dec_gain": dec_gain, "w_query": w_query, "w_key": w_key, "w_value": w_value, "w_proj": w_proj}


def normalize(values):
    average = lax.optimization_barrier(jnp.mean(values, axis=-1, keepdims=True))
    centered = values - average
    spread = lax.optimization_barrier(jnp.mean(centered * centered, axis=-1, keepdims=True))
    return centered * lax.rsqrt(spread + 1e-06)

def positions(first, count, width):
    index_values = (first + jnp.arange(count, dtype=jnp.int32)).astype(jnp.float32)
    freqs = 1.0 / 10000.0 ** (jnp.arange(width // 2, dtype=jnp.float32) / (width // 2))
    angle = index_values[:, None] * freqs[None, :]
    return jnp.concatenate([jnp.sin(angle), jnp.cos(angle)], axis=-1)

def head_attention(operands):
    query_head, key_head, value_head = operands
    block = math.gcd(query_head.shape[0], 1024)
    blocks = query_head.reshape(-1, block, query_head.shape[1])

    def one_block(query_block):
        scores = jnp.dot(query_block, key_head.T, preferred_element_type=jnp.float32) / math.sqrt(HD)
        top_score = lax.optimization_barrier(jnp.max(scores, axis=-1, keepdims=True))
        expo = jnp.exp(scores - top_score)
        summed = jnp.dot(expo.astype(jnp.bfloat16), value_head, preferred_element_type=jnp.float32)
        return (summed / lax.optimization_barrier(jnp.sum(expo, axis=-1, keepdims=True))).astype(jnp.bfloat16)
    return lax.map(one_block, blocks).reshape(query_head.shape)

def reference(enc_tokens, enc_gain, enc_bias, w_in, w_out, final_gain, w_embed, dest, mask_token, dec_gain, w_query, w_key, w_value, w_proj):
    token_values = enc_tokens.astype(jnp.float32)
    normed = (normalize(token_values) * enc_gain + enc_bias).astype(jnp.bfloat16)
    pre_act = jnp.einsum('ivd,df->ivf', normed.astype(jnp.float32), w_in.astype(jnp.float32))
    hidden = jax.nn.gelu(pre_act, approximate=False).astype(jnp.bfloat16)
    mixed = token_values + jnp.einsum('ivf,fd->ivd', hidden.astype(jnp.float32), w_out.astype(jnp.float32))
    encoded = (normalize(mixed) * final_gain).astype(jnp.bfloat16)
    embedded = jnp.einsum('ivd,de->ive', encoded.astype(jnp.float32), w_embed.astype(jnp.float32)).astype(jnp.bfloat16)
    targets = dest[:, :, 0].reshape(IMAGES, N_SEQ, VIS_DEV)
    matching = targets[:, :, :, None] == targets[:, :, None, :]
    ordering = jnp.arange(VIS_DEV, dtype=jnp.int32)
    before = ordering[None, :] < ordering[:, None]
    ranking = lax.optimization_barrier(jnp.sum(jnp.where(matching & before[None, None], 1, 0), axis=-1)).astype(jnp.int32)
    sources = jnp.arange(N_SEQ, dtype=jnp.int32)
    position = (targets * PATCH_DEV + sources[None, :, None] * MOST + ranking).reshape(IMAGES, VIS).astype(jnp.int32)
    image_index = jnp.arange(IMAGES, dtype=jnp.int32)[:, None]
    filled = jnp.zeros((IMAGES, PATCHES, DD), jnp.bfloat16).at[image_index, position].set(embedded)
    present = jnp.zeros((IMAGES, PATCHES), jnp.int32).at[image_index, position].set(1)
    dec_x = jnp.where(present[:, :, None] > 0, filled.astype(jnp.float32), mask_token.astype(jnp.float32)[None, None, :])
    dec_x = dec_x + positions(0, PATCHES, DD)[None]
    dec_norm = (normalize(dec_x) * dec_gain).astype(jnp.bfloat16)

    def project(weight):
        return jnp.einsum('ipd,dc->ipc', dec_norm.astype(jnp.float32), weight.astype(jnp.float32)).astype(jnp.bfloat16)

    def by_head(values):
        return values.reshape(IMAGES, PATCHES, HEADS, HD).transpose(0, 2, 1, 3).reshape(IMAGES * HEADS, PATCHES, HD)
    attended = lax.map(head_attention, (by_head(project(w_query)), by_head(project(w_key)), by_head(project(w_value))))
    attended = attended.reshape(IMAGES, HEADS, PATCHES, HD).transpose(0, 2, 1, 3).reshape(IMAGES, PATCHES, DH)
    output = dec_x + jnp.einsum('ipc,cd->ipd', attended.astype(jnp.float32), w_proj.astype(jnp.float32))
    return output.astype(jnp.bfloat16)
```

```python
import functools
import math

import jax
import jax.numpy as jnp
import numpy as np
from jax import lax
from jax.experimental import pallas as pl
from jax.experimental.pallas import tpu as pltpu
from jax.sharding import PartitionSpec as P

HD = 32
TILE = 128
BIG = -1e30
MESH = pl.DeviceIdType.MESH
F32 = jnp.float32
BF16 = jnp.bfloat16


def contract_last(left, right):
    return lax.dot_general(left, right, (((1,), (1,)), ((), ())), preferred_element_type=F32)


def matmul(left, right):
    return jnp.dot(left, right, preferred_element_type=F32)


def normalize(values):
    average = jnp.mean(values, axis=-1, keepdims=True)
    centered = values - average
    spread = jnp.mean(centered * centered, axis=-1, keepdims=True)
    return centered * lax.rsqrt(spread + 1e-06)


def iota(shape, dim):
    return lax.broadcasted_iota(jnp.int32, shape, dim)


def waves(count, scale, width):
    half = width // 2
    freqs = 1.0 / 10000.0 ** (np.arange(half, dtype=np.float64) / half)
    angle = (np.arange(count, dtype=np.float64) * scale)[:, None] * freqs[None, :]
    return np.concatenate([np.sin(angle), np.cos(angle)], axis=-1).astype(np.float32)


def turned(first, second):
    half = first.shape[-1] // 2
    sin_a, cos_a = first[:, :half], first[:, half:]
    sin_b, cos_b = second[:, :half], second[:, half:]
    return jnp.concatenate([sin_a * cos_b + cos_a * sin_b, cos_a * cos_b - sin_a * sin_b], axis=-1)


def picked(one_hot, table):
    high = table.astype(BF16)
    low = (table - high.astype(F32)).astype(BF16)
    return matmul(one_hot, high) + matmul(one_hot, low)


def kernel(
    cfg,
    tok_ref,
    gain_ref,
    bias_ref,
    w_in_hbm,
    w_out_hbm,
    final_ref,
    w_embed_hbm,
    dest_ref,
    mask_ref,
    dec_gain_ref,
    wq_ref,
    wk_ref,
    wv_ref,
    w_proj_ref,
    waves_hbm,
    near_ref,
    far_ref,
    rot_ref,
    perm_ref,
    out_ref,
    w_in,
    w_out,
    w_embed,
    wave_t,
    part_own,
    part_send,
    rs_recv,
    enc_all,
    e_all,
    a_src,
    a_y,
    a_mid,
    a_z,
    q_src,
    q_y,
    q_mid,
    q_z,
    kv,
    kt,
    kb,
    vt,
    res_recv,
    tile_pos,
    stat_w,
    pr_own,
    pr_send,
    pr_recv,
    local_sem,
    x_send,
    x_recv,
    y_send,
    y_recv,
    z_send,
    z_recv,
):
    nx, ny, nz, images, vis = cfg
    tiles = ny * nz
    cap = TILE // tiles
    rows = images * vis
    block_rows = rows // nx
    width = out_ref.shape[2]
    cols = wq_ref.shape[1]
    own_rows = TILE // nx
    seq = lax.axis_index("seq")
    mx = lax.axis_index("mp")
    z, y = seq // ny, seq % ny

    loads = []
    for number, (src, dst) in enumerate(
        ((w_in_hbm, w_in), (w_out_hbm, w_out), (w_embed_hbm, w_embed), (waves_hbm, wave_t))
    ):
        load = pltpu.make_async_copy(src, dst, local_sem.at[number])
        load.start()
        loads.append(load)

    def partner(axis, d):
        if axis == "x":
            index = lax.rem(mx + d, nx)
            return index, {"mp": index}
        if axis == "y":
            index = lax.rem(y + d, ny)
            return index, {"seq": z * ny + index}
        index = lax.rem(z + d, nz)
        return index, {"seq": index * ny + y}

    sizes = {"x": nx, "y": ny, "z": nz}
    places = {"x": mx, "y": y, "z": z}
    sems = {"x": (x_send, x_recv), "y": (y_send, y_recv), "z": (z_send, z_recv)}
    barrier = pltpu.get_barrier_semaphore()
    for axis in "xyz":
        for d in range(1, sizes[axis]):
            pl.semaphore_signal(barrier, inc=1, device_id=partner(axis, d)[1], device_id_type=MESH)

    pending = []

    def order(size):
        return sorted(range(1, size), key=lambda d: -min(d, size - d))

    def exchange(axis, group, source, target):
        size = sizes[axis]
        send, recv = sems[axis]
        for d in order(size):
            index, device = partner(axis, d)
            copy = pltpu.make_async_remote_copy(
                src_ref=source(index),
                dst_ref=target(places[axis], d),
                send_sem=send.at[group, d - 1],
                recv_sem=recv.at[group, d - 1],
                device_id=device,
                device_id_type=MESH,
            )
            copy.start()
            pending.append(copy)

        def arrived(d):
            sender, device = partner(axis, size - d)
            pltpu.make_async_remote_copy(
                src_ref=target(sender, d),
                dst_ref=target(sender, d),
                send_sem=send.at[group, d - 1],
                recv_sem=recv.at[group, d - 1],
                device_id=device,
                device_id_type=MESH,
            ).wait_recv()

        def all_arrived():
            for d in range(1, size):
                arrived(d)

        return all_arrived

    def part_of(ref, count):
        return lambda index, d=0: ref.at[pl.ds(pl.multiple_of(index * count, count), count)]

    tokens = tok_ref[...].astype(F32)
    normed = (normalize(tokens) * gain_ref[...][None, :] + bias_ref[...][None, :]).astype(BF16)
    loads[0].wait()
    pre = matmul(normed, w_in[...])
    hidden = (0.5 * pre * (1.0 + lax.erf(pre * math.sqrt(0.5)))).astype(BF16)
    loads[1].wait()
    partial = matmul(hidden, w_out[...])
    part_own[...] = partial
    part_send[...] = partial.astype(BF16)
    pl.semaphore_wait(barrier, (nx - 1) + (ny - 1) + (nz - 1))
    rs_done = exchange("x", 0, part_of(part_send, block_rows), lambda index, d: rs_recv.at[d - 1])

    dest_col = dest_ref[...]
    eye = iota((rows, rows), 0) == iota((rows, rows), 1)
    dest_row = jnp.sum(jnp.where(eye, dest_col, 0), axis=0, keepdims=True)
    same = (dest_col == dest_row) & (iota((rows, rows), 0) // vis == iota((rows, rows), 1) // vis)
    rank_col = jnp.sum(
        jnp.where(same & (iota((rows, rows), 1) < iota((rows, rows), 0)), 1, 0), axis=1, keepdims=True
    )
    rank_row = jnp.sum(
        jnp.where(same & (iota((rows, rows), 0) < iota((rows, rows), 1)), 1, 0), axis=0, keepdims=True
    )
    slot_col = dest_col * cap + rank_col
    hits = jnp.where(slot_col == iota((rows, TILE), 1), 1.0, 0.0)
    flag_rows = jnp.zeros((16, TILE), F32)
    for i in range(images):
        count = jnp.sum(hits[i * vis : (i + 1) * vis], axis=0, keepdims=True)
        flag_rows = jnp.where(iota((16, TILE), 0) == i, count, flag_rows)

    def flag_lanes(count):
        return lambda index, d=0: kb.at[:, pl.ds(pl.multiple_of(index * count, TILE), count)]

    kb[:, pl.ds(pl.multiple_of(seq * TILE, TILE), TILE)] = (flag_rows * BIG).astype(BF16)
    flags_y = exchange(
        "y", 0, lambda index: flag_lanes(TILE)(seq), lambda index, d: flag_lanes(TILE)(z * ny + index)
    )
    order_row = ((dest_row % ny) * nz + dest_row // ny) * cap + rank_row
    spread_f = jnp.where(order_row == iota((TILE, rows), 0), 1.0, 0.0)
    lane_image = iota((TILE, rows), 1) // vis
    spreads = [jnp.where(lane_image == i, spread_f, 0.0) for i in range(images)]
    taken = [jnp.sum(one, axis=1, keepdims=True) for one in spreads]
    spreads = [one.astype(BF16) for one in spreads]

    at_tile = jnp.where(dest_col == iota((rows, tiles), 1), 1.0, 0.0).astype(BF16)
    at_place = jnp.where(seq * cap + rank_col == iota((rows, TILE), 1), 1.0, 0.0).astype(BF16)
    vis_pos = turned(picked(at_tile, far_ref[...]), picked(at_place, near_ref[...]))
    tile_pos[...] = turned(near_ref[...], far_ref[pl.ds(seq, 1), :])

    mask = mask_ref[...].astype(F32)[None, :]
    dec_gain = dec_gain_ref[...][None, :]
    mask_mid = mask - jnp.mean(mask, axis=-1, keepdims=True)
    mask_spread = jnp.mean(mask_mid * mask_mid, axis=-1, keepdims=True) + 0.5
    weights = jnp.concatenate([wk_ref[...], wv_ref[...]], axis=1)
    kv_cols = 2 * cols
    eye_w = jnp.where(iota((kv_cols, kv_cols), 0) == iota((kv_cols, kv_cols), 1), 1.0, 0.0).astype(BF16)
    gained = contract_last(eye_w, weights) * dec_gain
    stat_w[0:kv_cols, :] = gained
    gain_sum = jnp.sum(gained, axis=1, keepdims=True)
    mask_sum = jnp.sum(gained * mask_mid, axis=1, keepdims=True)
    stat_rows = iota((16, width), 0)
    stat_w[kv_cols:, :] = jnp.where(stat_rows == 0, 1.0, jnp.where(stat_rows == 1, mask_mid, 0.0)) * (1.0 / width)
    lanes = wave_t.shape[1]
    loads[3].wait()
    half = width // 2

    def table_step(step, carry):
        turn = rot_ref[pl.ds(step, 1), :]
        sin_t, cos_t = turn[:, :half], turn[:, half:]
        sin_w, cos_w = stat_w[:, :half], stat_w[:, half:]
        rotated = jnp.concatenate(
            [(sin_w * cos_t - cos_w * sin_t).astype(BF16), (sin_w * sin_t + cos_w * cos_t).astype(BF16)], axis=1
        )
        found = matmul(rotated, wave_t[...])
        average = found[kv_cols : kv_cols + 1]
        spread = mask_spread + 2.0 * found[kv_cols + 1 : kv_cols + 2] - average * average
        scale = lax.rsqrt(jnp.maximum(spread, 0.0) + 1e-06)
        made = ((found[:kv_cols] + mask_sum - average * gain_sum) * scale).astype(BF16)
        where = pl.ds(pl.multiple_of(step * lanes, lanes), lanes)
        kt[:, where] = made[:cols]
        vt[:, where] = made[cols:]
        return carry

    steps = rot_ref.shape[0]
    cut = [0, steps * 3 // 8, steps * 6 // 8, steps]
    lax.fori_loop(cut[0], cut[1], table_step, 0)

    rs_done()
    mine = pl.ds(pl.multiple_of(mx * block_rows, block_rows), block_rows)
    mixed = tok_ref[mine, :].astype(F32) + part_own[mine, :]
    for d in range(nx - 1):
        mixed = mixed + rs_recv[d].astype(F32)
    enc_all[mine, :] = (normalize(mixed) * final_ref[...][None, :]).astype(BF16)
    enc_done = exchange(
        "x", 1, lambda index: part_of(enc_all, block_rows)(mx), lambda index, d: part_of(enc_all, block_rows)(index)
    )
    lax.fori_loop(cut[1], cut[2], table_step, 0)
    flags_y()
    flags_z = exchange(
        "z", 0, lambda index: flag_lanes(TILE * ny)(z), lambda index, d: flag_lanes(TILE * ny)(index)
    )
    loads[2].wait()
    enc_done()
    embedded = matmul(enc_all[...], w_embed[...]).astype(BF16)
    e_all[mx] = embedded
    e_done = exchange("x", 2, lambda index: e_all.at[mx], lambda index, d: e_all.at[index])
    ry, rz = nz * cap, ny * cap
    a_src[...] = jnp.concatenate([matmul(one, embedded) for one in spreads], axis=1).astype(BF16)

    def first_leg(group, src, mid):
        done = exchange("y", group, part_of(src, ry), part_of(mid, ry))
        mid[pl.ds(pl.multiple_of(y * ry, ry), ry), :] = src[pl.ds(pl.multiple_of(y * ry, ry), ry), :]
        return done

    def second_leg(group, mid, turned_ref, final):
        turned_ref[...] = matmul(perm_ref[...], mid[...]).astype(BF16)
        done = exchange("z", group, part_of(turned_ref, rz), part_of(final, rz))
        final[pl.ds(pl.multiple_of(z * rz, rz), rz), :] = turned_ref[pl.ds(pl.multiple_of(z * rz, rz), rz), :]
        return done

    a_first = first_leg(1, a_src, a_y)
    lax.fori_loop(cut[2], cut[3], table_step, 0)

    score_scale = math.log2(math.e) / math.sqrt(HD)
    mask_rows = (normalize(mask + tile_pos[...]) * dec_gain).astype(BF16)
    mask_query = matmul(mask_rows, wq_ref[...]) * score_scale

    e_done()
    full = jnp.concatenate([e_all[i] for i in range(nx)], axis=1).astype(F32)
    vis_rows = (normalize(full + vis_pos) * dec_gain).astype(BF16)
    vis_kv = jnp.concatenate([matmul(vis_rows, wv_ref[...]), matmul(vis_rows, wk_ref[...])], axis=1).astype(BF16)
    kv[0, pl.ds(pl.multiple_of(seq * vis, vis), vis), :] = vis_kv[:vis]
    kv[1, pl.ds(pl.multiple_of((y * nz + z) * vis, vis), vis), :] = vis_kv[vis:]
    query = (matmul(vis_rows, wq_ref[...]) * score_scale).astype(BF16)
    q_src[...] = jnp.concatenate(
        [matmul(one, query) for one in spreads]
        + [jnp.broadcast_to(one, (TILE, cols)) for one in taken],
        axis=1,
    ).astype(BF16)
    q_first = first_leg(2, q_src, q_y)
    kv0, kv1 = part_of(kv.at[0], vis), part_of(kv.at[1], vis)
    kv0_first = exchange("y", 3, lambda index: kv0(seq), lambda index, d: kv0(z * ny + index))
    kv1_first = exchange("z", 3, lambda index: kv1(y * nz + z), lambda index, d: kv1(y * nz + index))
    a_first()
    a_second = second_leg(1, a_y, a_mid, a_z)
    q_first()
    q_second = second_leg(2, q_y, q_mid, q_z)
    kv0_first()
    kv0_many = part_of(kv.at[0], vis * ny)
    kv0_second = exchange("z", 4, lambda index: kv0_many(z), lambda index, d: kv0_many(index))
    kv1_first()
    kv1_many = part_of(kv.at[1], vis * nz)
    kv1_second = exchange("y", 4, lambda index: kv1_many(y), lambda index, d: kv1_many(index))

    a_second()
    res_done = exchange("x", 3, part_of(a_z, own_rows), lambda index, d: res_recv.at[index])
    res_recv[mx] = a_z[pl.ds(pl.multiple_of(mx * own_rows, own_rows), own_rows), :]

    flags_z()
    q_second()
    lane = iota((TILE, cols), 1)
    head_masks = [jnp.where(lane // HD == h, 1.0, 0.0) for h in range(cols // HD)]
    heads = len(head_masks)
    found_q = q_z[...]
    states = []
    block = 1024 if tiles * TILE % 1024 == 0 else tiles * TILE
    stacked = []
    for i in range(images):
        present = found_q[:, (images + i) * cols : (images + i + 1) * cols].astype(F32)
        here = jnp.where(present > 0, found_q[:, i * cols : (i + 1) * cols].astype(F32), mask_query)
        stacked.append(jnp.concatenate([here * one for one in head_masks], axis=0).astype(BF16))

    def fold(state, scores, values_of):
        top, total, accum = state
        new_top = jnp.maximum(top, jnp.max(scores, axis=1, keepdims=True))
        fix = jnp.exp2(top - new_top)
        expo = jnp.exp2(scores - new_top)
        total = total * fix + jnp.sum(expo, axis=1, keepdims=True)
        accum = accum * fix + values_of(expo.astype(BF16))
        return new_top, total, accum

    for i in range(images):
        select = jnp.where(iota((heads * TILE, 16), 1) == i, 1.0, 0.0).astype(BF16)
        lookup = jnp.concatenate([stacked[i], select], axis=1)

        def masked_block(number, state):
            where = pl.ds(pl.multiple_of(number * block, block), block)
            scores = matmul(lookup, jnp.concatenate([kt[:, where], kb[:, where]], axis=0))
            return fold(state, scores, lambda expo: contract_last(expo, vt[:, where]))

        start = (
            jnp.full((heads * TILE, 1), BIG, F32),
            jnp.zeros((heads * TILE, 1), F32),
            jnp.zeros((heads * TILE, cols), F32),
        )
        states.append(lax.fori_loop(0, tiles * TILE // block, masked_block, start))

    vis_block = min(1024, tiles * vis)
    projected = []
    rs2 = []
    for i in range(images):
        (kv0_second if i == 0 else kv1_second)()
        lookup = jnp.concatenate([jnp.zeros_like(stacked[i]), stacked[i]], axis=1)

        def visible_block(number, state):
            pairs = kv[i, pl.ds(pl.multiple_of(number * vis_block, vis_block), vis_block), :]
            scores = contract_last(lookup, pairs)
            return fold(state, scores, lambda expo: matmul(expo, pairs)[:, :cols])

        top, total, accum = lax.fori_loop(0, tiles * vis // vis_block, visible_block, states[i])
        accum = accum / total
        attended = jnp.zeros((TILE, cols), F32)
        for h in range(heads):
            attended = attended + accum[h * TILE : (h + 1) * TILE] * head_masks[h]
        result = matmul(attended.astype(BF16), w_proj_ref[...])
        pr_own[i] = result
        pr_send[i] = result.astype(BF16)
        rs2.append(
            exchange("x", 4 + i, part_of(pr_send.at[i], own_rows), lambda index, d, i=i: pr_recv.at[d - 1, i])
        )

    res_done()
    tile_mine = pl.ds(pl.multiple_of(mx * own_rows, own_rows), own_rows)
    my_flags = q_z[tile_mine, :].astype(F32)
    my_pos = tile_pos[tile_mine, :]
    chunk = width // nx
    for i in range(images):
        rows_here = jnp.concatenate(
            [res_recv[j, :, i * chunk : (i + 1) * chunk] for j in range(nx)], axis=1
        ).astype(F32)
        start_lane = (images + i) * cols
        present = my_flags[:, start_lane : start_lane + 1]
        value = jnp.where(present > 0, rows_here, mask) + my_pos + pr_own[i, tile_mine, :]
        rs2[i]()
        for d in range(nx - 1):
            value = value + pr_recv[d, i].astype(F32)
        out_ref[i] = value.astype(BF16)
    for copy in pending:
        copy.wait_send()


def local(
    enc_tokens,
    enc_gain,
    enc_bias,
    w_in,
    w_out,
    final_gain,
    w_embed,
    dest,
    mask_token,
    dec_gain,
    w_query,
    w_key,
    w_value,
    w_proj,
):
    images, vis, model_width = enc_tokens.shape
    seq_count = lax.axis_size("seq")
    nx = lax.axis_size("mp")
    ny = math.isqrt(seq_count)
    nz = seq_count // ny
    width = mask_token.shape[0]
    cols = w_query.shape[1]
    cap = TILE // seq_count
    rows = images * vis
    own = TILE // nx
    patches = seq_count * TILE

    low = min(4, seq_count // 2)
    s_low, t, c = np.meshgrid(np.arange(low), np.arange(seq_count), np.arange(cap), indexing="ij")
    place = (s_low * cap + t * TILE + c).reshape(-1)
    wave_t = waves(int(place.max()) + 1, 1, width)[place].T.astype(jnp.bfloat16)
    near = waves(TILE, 1, width)
    far = waves(seq_count, TILE, width)
    rot = waves(seq_count // low, low * cap, width)
    zi, yi, ci = np.meshgrid(np.arange(nz), np.arange(ny), np.arange(cap), indexing="ij")
    perm = np.zeros((TILE, TILE), np.float32)
    perm[np.arange(TILE), ((yi * nz + zi) * cap + ci).reshape(-1)] = 1.0

    hbm = pl.BlockSpec(memory_space=pl.ANY)
    vmem = pl.BlockSpec(memory_space=pltpu.VMEM)
    block_rows = rows // nx
    dma = pltpu.SemaphoreType.DMA
    scratch = [
        pltpu.VMEM(w_in.shape, BF16),
        pltpu.VMEM(w_out.shape, BF16),
        pltpu.VMEM(w_embed.shape, BF16),
        pltpu.VMEM(wave_t.shape, BF16),
        pltpu.VMEM((rows, model_width), F32),
        pltpu.VMEM((rows, model_width), BF16),
        pltpu.VMEM((nx - 1, block_rows, model_width), BF16),
        pltpu.VMEM((rows, model_width), BF16),
        pltpu.VMEM((nx, rows, width // nx), BF16),
        *[pltpu.VMEM((TILE, images * width // nx), BF16)] * 4,
        *[pltpu.VMEM((TILE, 2 * images * cols), BF16)] * 4,
        pltpu.VMEM((images, seq_count * vis, 2 * cols), BF16),
        pltpu.VMEM((cols, patches), BF16),
        pltpu.VMEM((16, patches), BF16),
        pltpu.VMEM((cols, patches), BF16),
        pltpu.VMEM((nx, own, images * width // nx), BF16),
        pltpu.VMEM((TILE, width), F32),
        pltpu.VMEM((2 * cols + 16, width), F32),
        pltpu.VMEM((images, TILE, width), F32),
        pltpu.VMEM((images, TILE, width), BF16),
        pltpu.VMEM((nx - 1, images, own, width), BF16),
        dma((4,)),
        dma((6, nx - 1)),
        dma((6, nx - 1)),
        dma((5, ny - 1)),
        dma((5, ny - 1)),
        dma((5, nz - 1)),
        dma((5, nz - 1)),
    ]
    return pl.pallas_call(
        functools.partial(kernel, (nx, ny, nz, images, vis)),
        out_shape=jax.ShapeDtypeStruct((images, own, width), BF16),
        in_specs=[
            vmem, vmem, vmem, hbm, hbm, vmem, hbm, vmem, vmem, vmem, vmem, vmem, vmem, vmem,
            hbm, vmem, vmem, vmem, vmem,
        ],
        out_specs=vmem,
        scratch_shapes=scratch,
        compiler_params=pltpu.CompilerParams(
            collective_id=0, has_side_effects=True, vmem_limit_bytes=50 * 2**20
        ),
    )(
        enc_tokens.reshape(rows, model_width),
        enc_gain,
        enc_bias,
        w_in,
        w_out,
        final_gain,
        w_embed,
        dest.reshape(rows, 1),
        mask_token,
        dec_gain,
        w_query,
        w_key,
        w_value,
        w_proj,
        jnp.asarray(wave_t),
        jnp.asarray(near),
        jnp.asarray(far),
        jnp.asarray(rot),
        jnp.asarray(perm, BF16),
    )


def solution(mesh):
    placed = (
        P("dp", "seq", None),
        P(),
        P(),
        P(None, "mp"),
        P("mp", None),
        P(),
        P(None, "mp"),
        P("dp", "seq", None),
        P(),
        P(),
        P(None, "mp"),
        P(None, "mp"),
        P(None, "mp"),
        P("mp", None),
    )
    return jax.shard_map(
        local, mesh=mesh, in_specs=placed, out_specs=P("dp", ("seq", "mp"), None), check_vma=False
    )
```

```python
import functools
import math

import jax
import jax.numpy as jnp
import numpy as np
from jax import lax
from jax.experimental import pallas as pl
from jax.experimental.pallas import tpu as pltpu
from jax.sharding import PartitionSpec as P

HD = 32
TILE = 128
BIG = -1e30
MESH = pl.DeviceIdType.MESH
F32 = jnp.float32
BF16 = jnp.bfloat16


def contract_last(left, right):
    return lax.dot_general(left, right, (((1,), (1,)), ((), ())), preferred_element_type=F32)


def matmul(left, right):
    return jnp.dot(left, right, preferred_element_type=F32)


def normalize(values):
    average = jnp.mean(values, axis=-1, keepdims=True)
    centered = values - average
    spread = jnp.mean(centered * centered, axis=-1, keepdims=True)
    return centered * lax.rsqrt(spread + 1e-06)


def iota(shape, dim):
    return lax.broadcasted_iota(jnp.int32, shape, dim)


def waves(count, scale, width):
    half = width // 2
    freqs = 1.0 / 10000.0 ** (np.arange(half, dtype=np.float64) / half)
    angle = (np.arange(count, dtype=np.float64) * scale)[:, None] * freqs[None, :]
    return np.concatenate([np.sin(angle), np.cos(angle)], axis=-1).astype(np.float32)


def turned(first, second):
    half = first.shape[-1] // 2
    sin_a, cos_a = first[:, :half], first[:, half:]
    sin_b, cos_b = second[:, :half], second[:, half:]
    return jnp.concatenate([sin_a * cos_b + cos_a * sin_b, cos_a * cos_b - sin_a * sin_b], axis=-1)


def picked(one_hot, table):
    high = table.astype(BF16)
    low = (table - high.astype(F32)).astype(BF16)
    return matmul(one_hot, high) + matmul(one_hot, low)


def kernel(
    cfg,
    *refs,
):
    inputs, out_ref, held = refs[:19], refs[19], refs[20:39]
    (
        part_own,
        part_send,
        rs_recv,
        enc_all,
        e_all,
        a_src,
        a_y,
        a_mid,
        a_z,
        q_src,
        q_y,
        q_mid,
        q_z,
        kv,
        kt,
        kb,
        vt,
        res_recv,
        tile_pos,
        stat_w,
        f_y,
        f_z,
        taken_ref,
        wp_all,
        att_send,
        att_recv,
        local_sem,
        x_send,
        x_recv,
        y_send,
        y_recv,
        z_send,
        z_recv,
    ) = refs[39:]
    (
        tok_ref,
        gain_ref,
        bias_ref,
        w_in,
        w_out,
        w_proj_ref,
        dest_ref,
        far_ref,
        near_ref,
        mask_ref,
        dec_gain_ref,
        wk_ref,
        wv_ref,
        wave_t,
        rot_ref,
        final_ref,
        w_embed,
        perm_ref,
        wq_ref,
    ) = held
    nx, ny, nz, images, vis = cfg
    tiles = ny * nz
    cap = TILE // tiles
    rows = images * vis
    block_rows = rows // nx
    width = out_ref.shape[2]
    cols = wq_ref.shape[0]
    own_rows = TILE // nx
    seq = lax.axis_index("seq")
    mx = lax.axis_index("mp")
    z, y = seq // ny, seq % ny

    loads = []
    for number, (src, dst) in enumerate(zip(inputs, held)):
        load = pltpu.make_async_copy(src, dst, local_sem.at[number])
        load.start()
        loads.append(load)

    def loaded(first, last):
        for load in loads[first:last]:
            load.wait()

    def partner(axis, d):
        if axis == "x":
            index = lax.rem(mx + d, nx)
            return index, {"mp": index}
        if axis == "y":
            index = lax.rem(y + d, ny)
            return index, {"seq": z * ny + index}
        index = lax.rem(z + d, nz)
        return index, {"seq": index * ny + y}

    sizes = {"x": nx, "y": ny, "z": nz}
    places = {"x": mx, "y": y, "z": z}
    sems = {"x": (x_send, x_recv), "y": (y_send, y_recv), "z": (z_send, z_recv)}
    barrier = pltpu.get_barrier_semaphore()
    for axis in "xyz":
        for d in range(1, sizes[axis]):
            pl.semaphore_signal(barrier, inc=1, device_id=partner(axis, d)[1], device_id_type=MESH)

    pending = []

    def near_first(size):
        return sorted(range(size), key=lambda d: (min(d, size - d), d))

    def exchange(axis, group, source, target):
        size = sizes[axis]
        send, recv = sems[axis]
        for d in near_first(size)[:0:-1]:
            index, device = partner(axis, d)
            copy = pltpu.make_async_remote_copy(
                src_ref=source(index),
                dst_ref=target(places[axis], d),
                send_sem=send.at[group, d - 1],
                recv_sem=recv.at[group, d - 1],
                device_id=device,
                device_id_type=MESH,
            )
            copy.start()
            pending.append(copy)

        def arrived(steps=None):
            for d in near_first(size)[1:] if steps is None else steps:
                sender, device = partner(axis, size - d)
                pltpu.make_async_remote_copy(
                    src_ref=target(sender, d),
                    dst_ref=target(sender, d),
                    send_sem=send.at[group, d - 1],
                    recv_sem=recv.at[group, d - 1],
                    device_id=device,
                    device_id_type=MESH,
                ).wait_recv()

        return arrived

    def part_of(ref, count):
        return lambda index, d=0: ref.at[pl.ds(pl.multiple_of(index * count, count), count)]

    loaded(0, 3)
    tokens = tok_ref[...].astype(F32)
    normed = (normalize(tokens) * gain_ref[...][None, :] + bias_ref[...][None, :]).astype(BF16)
    loaded(3, 4)
    pre = matmul(normed, w_in[...])
    hidden = (0.5 * pre * (1.0 + lax.erf(pre * math.sqrt(0.5)))).astype(BF16)
    loaded(4, 5)
    partial = matmul(hidden, w_out[...])
    part_own[...] = partial
    part_send[...] = partial.astype(BF16)
    pl.semaphore_wait(barrier, (nx - 1) + (ny - 1) + (nz - 1))
    rs_done = exchange("x", 0, part_of(part_send, block_rows), lambda index, d: rs_recv.at[d - 1])
    loaded(5, 6)
    wp_all[mx] = w_proj_ref[...]
    wp_done = exchange("x", 4, lambda index: wp_all.at[mx], lambda index, d: wp_all.at[index])

    loaded(6, 15)
    dest_row = jnp.concatenate([dest_ref[i] for i in range(images)], axis=1)
    eye = iota((rows, rows), 0) == iota((rows, rows), 1)
    dest_col = jnp.sum(jnp.where(eye, dest_row, 0), axis=1, keepdims=True)
    same = (dest_col == dest_row) & (iota((rows, rows), 0) // vis == iota((rows, rows), 1) // vis)
    rank_col = jnp.sum(
        jnp.where(same & (iota((rows, rows), 1) < iota((rows, rows), 0)), 1, 0), axis=1, keepdims=True
    )
    rank_row = jnp.sum(
        jnp.where(same & (iota((rows, rows), 0) < iota((rows, rows), 1)), 1, 0), axis=0, keepdims=True
    )
    slot_col = dest_col * cap + rank_col
    hits = jnp.where(slot_col == iota((rows, TILE), 1), 1.0, 0.0)
    flag_rows = jnp.zeros((16, TILE), F32)
    for i in range(images):
        count = jnp.sum(hits[i * vis : (i + 1) * vis], axis=0, keepdims=True)
        flag_rows = jnp.where(iota((16, TILE), 0) == i, count, flag_rows)

    f_y[y] = (flag_rows * BIG).astype(BF16)
    flags_y = exchange("y", 0, lambda index: f_y.at[y], lambda index, d: f_y.at[index])
    order_row = ((dest_row % ny) * nz + dest_row // ny) * cap + rank_row
    spread_f = jnp.where(order_row == iota((TILE, rows), 0), 1.0, 0.0)
    lane_image = iota((TILE, rows), 1) // vis
    spreads = [jnp.where(lane_image == i, spread_f, 0.0) for i in range(images)]
    spreads = [one.astype(BF16) for one in spreads]

    at_tile = jnp.where(dest_col == iota((rows, tiles), 1), 1.0, 0.0).astype(BF16)
    at_place = jnp.where(seq * cap + rank_col == iota((rows, TILE), 1), 1.0, 0.0).astype(BF16)
    vis_pos = turned(picked(at_tile, far_ref[...]), picked(at_place, near_ref[...]))
    tile_pos[...] = turned(near_ref[...], far_ref[pl.ds(seq, 1), :])

    mask = mask_ref[...].astype(F32)[None, :]
    dec_gain = dec_gain_ref[...][None, :]
    mask_mid = mask - jnp.mean(mask, axis=-1, keepdims=True)
    mask_spread = jnp.mean(mask_mid * mask_mid, axis=-1, keepdims=True) + 0.5
    kv_cols = 2 * cols
    gained = jnp.concatenate([wk_ref[...], wv_ref[...]], axis=0).astype(F32) * dec_gain
    stat_w[0:kv_cols, :] = gained
    gain_sum = jnp.sum(gained, axis=1, keepdims=True)
    mask_sum = jnp.sum(gained * mask_mid, axis=1, keepdims=True)
    stat_rows = iota((16, width), 0)
    stat_w[kv_cols:, :] = jnp.where(stat_rows == 0, 1.0, jnp.where(stat_rows == 1, mask_mid, 0.0)) * (1.0 / width)
    lanes = wave_t.shape[1]
    half = width // 2

    def table_step(step, carry):
        turn = rot_ref[pl.ds(step, 1), :]
        sin_t, cos_t = turn[:, :half], turn[:, half:]
        sin_w, cos_w = stat_w[:, :half], stat_w[:, half:]
        rotated = jnp.concatenate(
            [(sin_w * cos_t - cos_w * sin_t).astype(BF16), (sin_w * sin_t + cos_w * cos_t).astype(BF16)], axis=1
        )
        found = matmul(rotated, wave_t[...])
        average = found[kv_cols : kv_cols + 1]
        spread = mask_spread + 2.0 * found[kv_cols + 1 : kv_cols + 2] - average * average
        scale = lax.rsqrt(jnp.maximum(spread, 0.0) + 1e-06)
        made = ((found[:kv_cols] + mask_sum - average * gain_sum) * scale).astype(BF16)
        where = pl.ds(pl.multiple_of(step * lanes, lanes), lanes)
        kt[:, where] = made[:cols]
        vt[:, where] = made[cols:]
        return carry

    steps = rot_ref.shape[0]
    cut = [0, steps * 3 // 8, steps * 6 // 8, steps]
    lax.fori_loop(cut[0], cut[1], table_step, 0)

    loaded(15, 19)
    rs_done()
    mine = pl.ds(pl.multiple_of(mx * block_rows, block_rows), block_rows)
    mixed = tok_ref[mine, :].astype(F32) + part_own[mine, :]
    for d in range(nx - 1):
        mixed = mixed + rs_recv[d].astype(F32)
    enc_all[mine, :] = (normalize(mixed) * final_ref[...][None, :]).astype(BF16)
    enc_done = exchange(
        "x", 1, lambda index: part_of(enc_all, block_rows)(mx), lambda index, d: part_of(enc_all, block_rows)(index)
    )
    lax.fori_loop(cut[1], cut[2], table_step, 0)
    flags_y()
    joined = [f_y[i].astype(F32)[:images] for i in range(ny)]
    if ny * images < 16:
        joined.append(jnp.zeros((16 - ny * images, TILE), F32))
    f_z[z] = jnp.concatenate(joined, axis=0).astype(BF16)
    flags_z = exchange("z", 0, lambda index: f_z.at[z], lambda index, d: f_z.at[index])
    enc_done()
    embedded = matmul(enc_all[...], w_embed[...]).astype(BF16)
    e_all[mx] = embedded
    e_done = exchange("x", 2, lambda index: e_all.at[mx], lambda index, d: e_all.at[index])
    ry, rz = nz * cap, ny * cap
    a_src[...] = jnp.concatenate([matmul(one, embedded) for one in spreads], axis=1).astype(BF16)

    def first_leg(group, src, mid):
        done = exchange("y", group, part_of(src, ry), part_of(mid, ry))
        mid[pl.ds(pl.multiple_of(y * ry, ry), ry), :] = src[pl.ds(pl.multiple_of(y * ry, ry), ry), :]
        return done

    def second_leg(group, mid, turned_ref, final):
        turned_ref[...] = matmul(perm_ref[...], mid[...]).astype(BF16)
        done = exchange("z", group, part_of(turned_ref, rz), part_of(final, rz))
        final[pl.ds(pl.multiple_of(z * rz, rz), rz), :] = turned_ref[pl.ds(pl.multiple_of(z * rz, rz), rz), :]
        return done

    a_first = first_leg(1, a_src, a_y)
    lax.fori_loop(cut[2], cut[3], table_step, 0)

    score_scale = math.log2(math.e) / math.sqrt(HD)
    mask_rows = (normalize(mask + tile_pos[...]) * dec_gain).astype(BF16)
    mask_query = contract_last(mask_rows, wq_ref[...]) * score_scale

    e_done()
    full = jnp.concatenate([e_all[i] for i in range(nx)], axis=1).astype(F32)
    vis_rows = (normalize(full + vis_pos) * dec_gain).astype(BF16)
    vis_kv = contract_last(vis_rows, jnp.concatenate([wv_ref[...], wk_ref[...]], axis=0)).astype(BF16)
    for i in range(images):
        kv[i, :vis, :] = vis_kv[i * vis : (i + 1) * vis]
    axes = [("y", "z"), ("z", "y")]
    firsts, seconds = [], [[] for _ in range(images)]

    def slots(i, first, last, outer=0):
        lead = outer * sizes[axes[i][0]]
        return kv.at[i, (lead + first) * vis : (lead + last) * vis]

    def place_of(axis, d):
        return near_first(sizes[axis]).index(d)

    for i in range(images):
        one, two = axes[i]
        firsts.append(
            exchange(
                one,
                3,
                lambda index, i=i: slots(i, 0, 1),
                lambda index, d, i=i, one=one: slots(i, place_of(one, d), place_of(one, d) + 1),
            )
        )

    def forward(i, group, first, last):
        two = axes[i][1]
        seconds[i].append(
            exchange(
                two,
                group,
                lambda index: slots(i, first, last),
                lambda index, d: slots(i, first, last, place_of(two, d)),
            )
        )

    def cuts(size):
        return [(1, 3), (3, 5), (5, 8)] if size == 8 else [(1, size)]

    query = (contract_last(vis_rows, wq_ref[...]) * score_scale).astype(BF16)
    q_src[...] = jnp.concatenate([matmul(one, query) for one in spreads], axis=1).astype(BF16)
    q_first = first_leg(2, q_src, q_y)
    a_first()
    a_second = second_leg(1, a_y, a_mid, a_z)
    for i in range(images):
        forward(i, 4, 0, 1)
    for number in range(len(cuts(ny))):
        for i in range(images)[::-1]:
            if number == 0 and i == 0:
                q_first()
                q_second = second_leg(2, q_y, q_mid, q_z)
            size = sizes[axes[i][0]]
            first, last = cuts(size)[number]
            firsts[i](near_first(size)[first:last])
            forward(i, 5 + number, first, last)
    a_second()
    res_done = exchange("x", 3, part_of(a_z, own_rows), lambda index, d: res_recv.at[index])
    res_recv[mx] = a_z[pl.ds(pl.multiple_of(mx * own_rows, own_rows), own_rows), :]

    flags_z()
    bias_row, bias_from = iota((ny * 16, 16), 0), iota((ny * 16, 16), 1)
    unpack = jnp.where(
        (bias_row % 16 < images) & (bias_from == (bias_row // 16) * images + bias_row % 16), 1.0, 0.0
    ).astype(BF16)
    for zs in range(nz):
        part = matmul(unpack, f_z[zs]).astype(BF16)
        for ys in range(ny):
            kb[:, (zs * ny + ys) * TILE : (zs * ny + ys + 1) * TILE] = part[ys * 16 : (ys + 1) * 16]
    every_flag = jnp.concatenate([f_z[zs] for zs in range(nz)], axis=0)
    slot_row, slot_from = iota((TILE, nz * 16), 0), iota((TILE, nz * 16), 1)
    source_row = slot_row // cap
    here_lane = iota((TILE, TILE), 1) == seq * cap + iota((TILE, TILE), 0) % cap
    presents = []
    for i in range(images):
        choose = jnp.where(slot_from == (source_row // ny) * 16 + (source_row % ny) * images + i, 1.0, 0.0)
        seen = jnp.where(here_lane, matmul(choose.astype(BF16), every_flag), 0.0)
        presents.append(jnp.where(jnp.sum(seen, axis=1, keepdims=True) < -1.0, 1.0, 0.0))
    taken_ref[...] = jnp.concatenate([jnp.broadcast_to(one, (TILE, TILE)) for one in presents], axis=1)
    q_second()
    lane = iota((TILE, cols), 1)
    head_masks = [jnp.where(lane // HD == h, 1.0, 0.0) for h in range(cols // HD)]
    heads = len(head_masks)
    found_q = q_z[...]
    block = math.gcd(2048, tiles * TILE)
    lookups = []
    stacked = []
    for i in range(images):
        here = jnp.where(presents[i] > 0, found_q[:, i * cols : (i + 1) * cols].astype(F32), mask_query)
        stacked.append(jnp.concatenate([here * one for one in head_masks], axis=0).astype(BF16))

    def fold(state, scores, values_of):
        top, total, accum = state
        new_top = jnp.maximum(top, jnp.max(scores, axis=1, keepdims=True))
        fix = jnp.exp2(top - new_top)
        expo = jnp.exp2(scores - new_top)
        total = total * fix + jnp.sum(expo, axis=1, keepdims=True)
        accum = accum * fix + values_of(expo.astype(BF16))
        return new_top, total, accum

    for i in range(images):
        select = jnp.where(iota((heads * TILE, 16), 1) == i, 1.0, 0.0).astype(BF16)
        lookups.append(jnp.concatenate([stacked[i], select], axis=1))

    def masked_block(number, states):
        where = pl.ds(pl.multiple_of(number * block, block), block)
        keys = jnp.concatenate([kt[:, where], kb[:, where]], axis=0)
        scores = [matmul(one, keys) for one in lookups]
        return tuple(
            fold(state, one, lambda expo: contract_last(expo, vt[:, where])) for state, one in zip(states, scores)
        )

    start = (
        jnp.full((heads * TILE, 1), BIG, F32),
        jnp.zeros((heads * TILE, 1), F32),
        jnp.zeros((heads * TILE, cols), F32),
    )
    states = lax.fori_loop(0, tiles * TILE // block, masked_block, (start,) * images)

    lookups = [jnp.concatenate([jnp.zeros_like(one), one], axis=1) for one in stacked]

    def visible(states, first, last):
        spans = [slice(first * sizes[axes[i][0]] * vis, last * sizes[axes[i][0]] * vis) for i in range(images)]
        scores = [contract_last(lookups[i], kv[i, spans[i], :]) for i in range(images)]
        return [
            fold(states[i], scores[i], lambda expo, i=i: matmul(expo, kv[i, spans[i], :])[:, :cols])
            for i in range(images)
        ]

    near = 5 if nz == 8 else 1
    for first, last in ((0, near), (near, nz)):
        for i in range(images):
            for second in seconds[i]:
                second(near_first(sizes[axes[i][1]])[max(first, 1) : last])
        states = visible(states, first, last)
    gathered = []
    for i in range(images):
        top, total, accum = states[i]
        accum = accum / total
        attended = jnp.zeros((TILE, cols), F32)
        for h in range(heads):
            attended = attended + accum[h * TILE : (h + 1) * TILE] * head_masks[h]
        gathered.append(attended)
    att_send[...] = jnp.concatenate(gathered, axis=1).astype(BF16)
    att_done = exchange("x", 5, part_of(att_send, own_rows), lambda index, d: att_recv.at[index])
    tile_mine = pl.ds(pl.multiple_of(mx * own_rows, own_rows), own_rows)
    att_recv[mx] = att_send[tile_mine, :]

    res_done()
    my_pos = tile_pos[tile_mine, :]
    chunk = width // nx
    bases = []
    for i in range(images):
        rows_here = jnp.concatenate(
            [res_recv[j, :, i * chunk : (i + 1) * chunk] for j in range(nx)], axis=1
        ).astype(F32)
        present = taken_ref[tile_mine, i * TILE : i * TILE + 1]
        bases.append(jnp.where(present > 0, rows_here, mask) + my_pos)
    wp_done()
    att_done()
    sums = jnp.concatenate(bases, axis=0)
    for j in range(nx):
        pieces = [att_recv[j, :, i * cols : (i + 1) * cols] for i in range(images)]
        sums = sums + matmul(jnp.concatenate(pieces, axis=0), wp_all[j])
    for i in range(images):
        out_ref[i] = sums[i * own_rows : (i + 1) * own_rows].astype(BF16)
    for copy in pending:
        copy.wait_send()


def local(
    enc_tokens,
    enc_gain,
    enc_bias,
    w_in,
    w_out,
    final_gain,
    w_embed,
    dest,
    mask_token,
    dec_gain,
    w_query,
    w_key,
    w_value,
    w_proj,
):
    images, vis, model_width = enc_tokens.shape
    seq_count = lax.axis_size("seq")
    nx = lax.axis_size("mp")
    ny = math.isqrt(seq_count)
    nz = seq_count // ny
    width = mask_token.shape[0]
    cols = w_query.shape[1]
    cap = TILE // seq_count
    rows = images * vis
    own = TILE // nx
    patches = seq_count * TILE

    low = min(4, seq_count // 2)
    s_low, t, c = np.meshgrid(np.arange(low), np.arange(seq_count), np.arange(cap), indexing="ij")
    place = (s_low * cap + t * TILE + c).reshape(-1)
    wave_t = waves(int(place.max()) + 1, 1, width)[place].T.astype(jnp.bfloat16)
    near = waves(TILE, 1, width)
    far = waves(seq_count, TILE, width)
    rot = waves(seq_count // low, low * cap, width)
    zi, yi, ci = np.meshgrid(np.arange(nz), np.arange(ny), np.arange(cap), indexing="ij")
    perm = np.zeros((TILE, TILE), np.float32)
    perm[np.arange(TILE), ((yi * nz + zi) * cap + ci).reshape(-1)] = 1.0

    hbm = pl.BlockSpec(memory_space=pltpu.HBM)
    vmem = pl.BlockSpec(memory_space=pltpu.VMEM)
    operands = (
        enc_tokens.reshape(rows, model_width),
        enc_gain,
        enc_bias,
        w_in,
        w_out,
        w_proj,
        dest.transpose(0, 2, 1),
        jnp.asarray(far),
        jnp.asarray(near),
        mask_token,
        dec_gain,
        w_key.T,
        w_value.T,
        jnp.asarray(wave_t),
        jnp.asarray(rot),
        final_gain,
        w_embed,
        jnp.asarray(perm, BF16),
        w_query.T,
    )
    block_rows = rows // nx
    dma = pltpu.SemaphoreType.DMA
    scratch = [
        *[pltpu.VMEM(operand.shape, operand.dtype) for operand in operands],
        pltpu.VMEM((rows, model_width), F32),
        pltpu.VMEM((rows, model_width), BF16),
        pltpu.VMEM((nx - 1, block_rows, model_width), BF16),
        pltpu.VMEM((rows, model_width), BF16),
        pltpu.VMEM((nx, rows, width // nx), BF16),
        *[pltpu.VMEM((TILE, images * width // nx), BF16)] * 4,
        *[pltpu.VMEM((TILE, images * cols), BF16)] * 4,
        pltpu.VMEM((images, seq_count * vis, 2 * cols), BF16),
        pltpu.VMEM((cols, patches), BF16),
        pltpu.VMEM((16, patches), BF16),
        pltpu.VMEM((cols, patches), BF16),
        pltpu.VMEM((nx, own, images * width // nx), BF16),
        pltpu.VMEM((TILE, width), F32),
        pltpu.VMEM((2 * cols + 16, width), F32),
        pltpu.VMEM((ny, 16, TILE), BF16),
        pltpu.VMEM((nz, 16, TILE), BF16),
        pltpu.VMEM((TILE, images * TILE), F32),
        pltpu.VMEM((nx, cols, width), BF16),
        pltpu.VMEM((TILE, images * cols), BF16),
        pltpu.VMEM((nx, own, images * cols), BF16),
        dma((len(operands),)),
        dma((6, nx - 1)),
        dma((6, nx - 1)),
        dma((8, ny - 1)),
        dma((8, ny - 1)),
        dma((8, nz - 1)),
        dma((8, nz - 1)),
    ]
    return pl.pallas_call(
        functools.partial(kernel, (nx, ny, nz, images, vis)),
        out_shape=pltpu.VMEM((images, own, width), BF16),
        in_specs=[hbm] * len(operands),
        out_specs=vmem,
        scratch_shapes=scratch,
        compiler_params=pltpu.CompilerParams(
            collective_id=0, has_side_effects=True, vmem_limit_bytes=63300000
        ),
    )(*operands)


def solution(mesh):
    placed = (
        P("dp", "seq", None),
        P(),
        P(),
        P(None, "mp"),
        P("mp", None),
        P(),
        P(None, "mp"),
        P("dp", "seq", None),
        P(),
        P(),
        P(None, "mp"),
        P(None, "mp"),
        P(None, "mp"),
        P("mp", None),
    )
    return jax.shard_map(
        local, mesh=mesh, in_specs=placed, out_specs=P("dp", ("seq", "mp"), None), check_vma=False
    )
```

```python
import functools
import math

import jax
import jax.numpy as jnp
import numpy as np
from jax import lax
from jax.experimental import pallas as pl
from jax.experimental.pallas import tpu as pltpu
from jax.sharding import PartitionSpec as P

HD = 32
TILE = 128
BIG = -1e30
MESH = pl.DeviceIdType.MESH
F32 = jnp.float32
BF16 = jnp.bfloat16


def contract_last(left, right):
    return lax.dot_general(left, right, (((1,), (1,)), ((), ())), preferred_element_type=F32)


def matmul(left, right):
    return jnp.dot(left, right, preferred_element_type=F32)


def normalize(values):
    average = jnp.mean(values, axis=-1, keepdims=True)
    centered = values - average
    spread = jnp.mean(centered * centered, axis=-1, keepdims=True)
    return centered * lax.rsqrt(spread + 1e-06)


def iota(shape, dim):
    return lax.broadcasted_iota(jnp.int32, shape, dim)


def waves(count, scale, width):
    half = width // 2
    freqs = 1.0 / 10000.0 ** (np.arange(half, dtype=np.float64) / half)
    angle = (np.arange(count, dtype=np.float64) * scale)[:, None] * freqs[None, :]
    return np.concatenate([np.sin(angle), np.cos(angle)], axis=-1).astype(np.float32)


def turned(first, second):
    half = first.shape[-1] // 2
    sin_a, cos_a = first[:, :half], first[:, half:]
    sin_b, cos_b = second[:, :half], second[:, half:]
    return jnp.concatenate([sin_a * cos_b + cos_a * sin_b, cos_a * cos_b - sin_a * sin_b], axis=-1)


def picked(one_hot, table):
    high = table.astype(BF16)
    low = (table - high.astype(F32)).astype(BF16)
    return matmul(one_hot, high) + matmul(one_hot, low)


def kernel(
    cfg,
    *refs,
):
    inputs, out_ref, held = refs[:19], refs[19], refs[20:39]
    (
        part_own,
        part_send,
        rs_recv,
        enc_all,
        e_all,
        a_src,
        a_y,
        a_mid,
        a_z,
        q_src,
        q_y,
        q_mid,
        q_z,
        kv,
        kt,
        kb,
        vt,
        res_recv,
        tile_pos,
        stat_w,
        f_y,
        f_z,
        taken_ref,
        wp_all,
        att_send,
        att_recv,
        local_sem,
        x_send,
        x_recv,
        y_send,
        y_recv,
        z_send,
        z_recv,
    ) = refs[39:]
    (
        tok_ref,
        gain_ref,
        bias_ref,
        w_in,
        w_out,
        w_proj_ref,
        dest_ref,
        far_ref,
        near_ref,
        mask_ref,
        dec_gain_ref,
        wk_ref,
        wv_ref,
        wave_t,
        rot_ref,
        final_ref,
        w_embed,
        perm_ref,
        wq_ref,
    ) = held
    nx, ny, nz, images, vis = cfg
    tiles = ny * nz
    cap = TILE // tiles
    rows = images * vis
    block_rows = rows // nx
    width = out_ref.shape[2]
    cols = wq_ref.shape[0]
    own_rows = TILE // nx
    seq = lax.axis_index("seq")
    mx = lax.axis_index("mp")
    z, y = seq // ny, seq % ny

    loads = []
    for number, (src, dst) in enumerate(zip(inputs, held)):
        loads.append(pltpu.make_async_copy(src, dst, local_sem.at[number]))

    def load_now(first, last):
        for load in loads[first:last]:
            load.start()

    load_now(0, 5)

    def loaded(first, last):
        for load in loads[first:last]:
            load.wait()

    def partner(axis, d):
        if axis == "x":
            index = lax.rem(mx + d, nx)
            return index, {"mp": index}
        if axis == "y":
            index = lax.rem(y + d, ny)
            return index, {"seq": z * ny + index}
        index = lax.rem(z + d, nz)
        return index, {"seq": index * ny + y}

    sizes = {"x": nx, "y": ny, "z": nz}
    places = {"x": mx, "y": y, "z": z}
    sems = {"x": (x_send, x_recv), "y": (y_send, y_recv), "z": (z_send, z_recv)}
    barrier = pltpu.get_barrier_semaphore()
    for axis in "xyz":
        for d in range(1, sizes[axis]):
            pl.semaphore_signal(barrier, inc=1, device_id=partner(axis, d)[1], device_id_type=MESH)

    pending = []

    def near_first(size):
        return sorted(range(size), key=lambda d: (min(d, size - d), d))

    def exchange(axis, group, source, target):
        size = sizes[axis]
        send, recv = sems[axis]
        for d in near_first(size)[:0:-1]:
            index, device = partner(axis, d)
            copy = pltpu.make_async_remote_copy(
                src_ref=source(index),
                dst_ref=target(places[axis], d),
                send_sem=send.at[group, d - 1],
                recv_sem=recv.at[group, d - 1],
                device_id=device,
                device_id_type=MESH,
            )
            copy.start()
            pending.append(copy)

        def arrived(steps=None):
            for d in near_first(size)[1:] if steps is None else steps:
                sender, device = partner(axis, size - d)
                pltpu.make_async_remote_copy(
                    src_ref=target(sender, d),
                    dst_ref=target(sender, d),
                    send_sem=send.at[group, d - 1],
                    recv_sem=recv.at[group, d - 1],
                    device_id=device,
                    device_id_type=MESH,
                ).wait_recv()

        return arrived

    def part_of(ref, count):
        return lambda index, d=0: ref.at[pl.ds(pl.multiple_of(index * count, count), count)]

    load_now(5, len(loads))
    loaded(0, 3)
    tokens = tok_ref[...].astype(F32)
    normed = (normalize(tokens) * gain_ref[...][None, :] + bias_ref[...][None, :]).astype(BF16)
    loaded(3, 4)
    pre = matmul(normed, w_in[...])
    hidden = (0.5 * pre * (1.0 + lax.erf(pre * math.sqrt(0.5)))).astype(BF16)
    loaded(4, 5)
    partial = matmul(hidden, w_out[...])
    part_own[...] = partial
    part_send[...] = partial.astype(BF16)
    pl.semaphore_wait(barrier, (nx - 1) + (ny - 1) + (nz - 1))
    rs_done = exchange("x", 0, part_of(part_send, block_rows), lambda index, d: rs_recv.at[d - 1])
    loaded(5, 6)
    wp_all[mx] = w_proj_ref[...]
    wp_done = exchange("x", 4, lambda index: wp_all.at[mx], lambda index, d: wp_all.at[index])

    loaded(6, 15)
    dest_row = jnp.concatenate([dest_ref[i] for i in range(images)], axis=1)
    eye = iota((rows, rows), 0) == iota((rows, rows), 1)
    dest_col = jnp.sum(jnp.where(eye, dest_row, 0), axis=1, keepdims=True)
    same = (dest_col == dest_row) & (iota((rows, rows), 0) // vis == iota((rows, rows), 1) // vis)
    rank_col = jnp.sum(
        jnp.where(same & (iota((rows, rows), 1) < iota((rows, rows), 0)), 1, 0), axis=1, keepdims=True
    )
    rank_row = jnp.sum(
        jnp.where(same & (iota((rows, rows), 0) < iota((rows, rows), 1)), 1, 0), axis=0, keepdims=True
    )
    slot_col = dest_col * cap + rank_col
    hits = jnp.where(slot_col == iota((rows, TILE), 1), 1.0, 0.0)
    flag_rows = jnp.zeros((16, TILE), F32)
    for i in range(images):
        count = jnp.sum(hits[i * vis : (i + 1) * vis], axis=0, keepdims=True)
        flag_rows = jnp.where(iota((16, TILE), 0) == i, count, flag_rows)

    f_y[y] = (flag_rows * BIG).astype(BF16)
    flags_y = exchange("y", 0, lambda index: f_y.at[y], lambda index, d: f_y.at[index])
    order_row = ((dest_row % ny) * nz + dest_row // ny) * cap + rank_row
    spread_f = jnp.where(order_row == iota((TILE, rows), 0), 1.0, 0.0)
    lane_image = iota((TILE, rows), 1) // vis
    spreads = [jnp.where(lane_image == i, spread_f, 0.0) for i in range(images)]
    spreads = [one.astype(BF16) for one in spreads]

    at_tile = jnp.where(dest_col == iota((rows, tiles), 1), 1.0, 0.0).astype(BF16)
    at_place = jnp.where(seq * cap + rank_col == iota((rows, TILE), 1), 1.0, 0.0).astype(BF16)
    vis_pos = turned(picked(at_tile, far_ref[...]), picked(at_place, near_ref[...]))
    tile_pos[...] = turned(near_ref[...], far_ref[pl.ds(seq, 1), :])

    mask = mask_ref[...].astype(F32)[None, :]
    dec_gain = dec_gain_ref[...][None, :]
    mask_mid = mask - jnp.mean(mask, axis=-1, keepdims=True)
    mask_spread = jnp.mean(mask_mid * mask_mid, axis=-1, keepdims=True) + 0.5
    kv_cols = 2 * cols
    gained = jnp.concatenate([wk_ref[...], wv_ref[...]], axis=0).astype(F32) * dec_gain
    stat_w[0:kv_cols, :] = gained
    gain_sum = jnp.sum(gained, axis=1, keepdims=True)
    mask_sum = jnp.sum(gained * mask_mid, axis=1, keepdims=True)
    stat_rows = iota((16, width), 0)
    stat_w[kv_cols:, :] = jnp.where(stat_rows == 0, 1.0, jnp.where(stat_rows == 1, mask_mid, 0.0)) * (1.0 / width)
    lanes = wave_t.shape[1]
    half = width // 2

    def table_step(step, carry):
        turn = rot_ref[pl.ds(step, 1), :]
        sin_t, cos_t = turn[:, :half], turn[:, half:]
        sin_w, cos_w = stat_w[:, :half], stat_w[:, half:]
        rotated = jnp.concatenate(
            [(sin_w * cos_t - cos_w * sin_t).astype(BF16), (sin_w * sin_t + cos_w * cos_t).astype(BF16)], axis=1
        )
        found = matmul(rotated, wave_t[...])
        average = found[kv_cols : kv_cols + 1]
        spread = mask_spread + 2.0 * found[kv_cols + 1 : kv_cols + 2] - average * average
        scale = lax.rsqrt(jnp.maximum(spread, 0.0) + 1e-06)
        made = ((found[:kv_cols] + mask_sum - average * gain_sum) * scale).astype(BF16)
        where = pl.ds(pl.multiple_of(step * lanes, lanes), lanes)
        kt[:, where] = made[:cols]
        vt[:, where] = made[cols:]
        return carry

    steps = rot_ref.shape[0]
    cut = [0, steps * 3 // 8, steps * 6 // 8, steps]
    lax.fori_loop(cut[0], cut[1], table_step, 0)

    loaded(15, 19)
    rs_done()
    mine = pl.ds(pl.multiple_of(mx * block_rows, block_rows), block_rows)
    mixed = tok_ref[mine, :].astype(F32) + part_own[mine, :]
    for d in range(nx - 1):
        mixed = mixed + rs_recv[d].astype(F32)
    enc_all[mine, :] = (normalize(mixed) * final_ref[...][None, :]).astype(BF16)
    enc_done = exchange(
        "x", 1, lambda index: part_of(enc_all, block_rows)(mx), lambda index, d: part_of(enc_all, block_rows)(index)
    )
    lax.fori_loop(cut[1], cut[2], table_step, 0)
    flags_y()
    joined = [f_y[i].astype(F32)[:images] for i in range(ny)]
    if ny * images < 16:
        joined.append(jnp.zeros((16 - ny * images, TILE), F32))
    f_z[z] = jnp.concatenate(joined, axis=0).astype(BF16)
    flags_z = exchange("z", 0, lambda index: f_z.at[z], lambda index, d: f_z.at[index])
    enc_done()
    embedded = matmul(enc_all[...], w_embed[...]).astype(BF16)
    e_all[mx] = embedded
    e_done = exchange("x", 2, lambda index: e_all.at[mx], lambda index, d: e_all.at[index])
    ry, rz = nz * cap, ny * cap
    a_src[...] = jnp.concatenate([matmul(one, embedded) for one in spreads], axis=1).astype(BF16)

    def first_leg(group, src, mid):
        done = exchange("y", group, part_of(src, ry), part_of(mid, ry))
        mid[pl.ds(pl.multiple_of(y * ry, ry), ry), :] = src[pl.ds(pl.multiple_of(y * ry, ry), ry), :]
        return done

    def second_leg(group, mid, turned_ref, final):
        turned_ref[...] = matmul(perm_ref[...], mid[...]).astype(BF16)
        done = exchange("z", group, part_of(turned_ref, rz), part_of(final, rz))
        final[pl.ds(pl.multiple_of(z * rz, rz), rz), :] = turned_ref[pl.ds(pl.multiple_of(z * rz, rz), rz), :]
        return done

    a_first = first_leg(1, a_src, a_y)
    lax.fori_loop(cut[2], cut[3], table_step, 0)

    score_scale = math.log2(math.e) / math.sqrt(HD)
    mask_rows = (normalize(mask + tile_pos[...]) * dec_gain).astype(BF16)
    mask_query = contract_last(mask_rows, wq_ref[...]) * score_scale

    e_done()
    full = jnp.concatenate([e_all[i] for i in range(nx)], axis=1).astype(F32)
    vis_rows = (normalize(full + vis_pos) * dec_gain).astype(BF16)
    vis_kv = contract_last(vis_rows, jnp.concatenate([wv_ref[...], wk_ref[...]], axis=0)).astype(BF16)
    for i in range(images):
        kv[i, :vis, :] = vis_kv[i * vis : (i + 1) * vis]
    axes = [("y", "z"), ("z", "y")]
    firsts, seconds = [], [[] for _ in range(images)]

    def slots(i, first, last, outer=0):
        lead = outer * sizes[axes[i][0]]
        return kv.at[i, (lead + first) * vis : (lead + last) * vis]

    def place_of(axis, d):
        return near_first(sizes[axis]).index(d)

    for i in range(images):
        one, two = axes[i]
        firsts.append(
            exchange(
                one,
                3,
                lambda index, i=i: slots(i, 0, 1),
                lambda index, d, i=i, one=one: slots(i, place_of(one, d), place_of(one, d) + 1),
            )
        )

    def forward(i, group, first, last):
        two = axes[i][1]
        seconds[i].append(
            exchange(
                two,
                group,
                lambda index: slots(i, first, last),
                lambda index, d: slots(i, first, last, place_of(two, d)),
            )
        )

    def cuts(size):
        return [(1, 3), (3, 5), (5, 8)] if size == 8 else [(1, size)]

    query = (contract_last(vis_rows, wq_ref[...]) * score_scale).astype(BF16)
    q_src[...] = jnp.concatenate([matmul(one, query) for one in spreads], axis=1).astype(BF16)
    q_first = first_leg(2, q_src, q_y)
    a_first()
    a_second = second_leg(1, a_y, a_mid, a_z)
    for i in range(images):
        forward(i, 4, 0, 1)
    for number in range(len(cuts(ny))):
        for i in range(images)[::-1]:
            if number == 0 and i == 0:
                q_first()
                q_second = second_leg(2, q_y, q_mid, q_z)
            size = sizes[axes[i][0]]
            first, last = cuts(size)[number]
            firsts[i](near_first(size)[first:last])
            forward(i, 5 + number, first, last)
    a_second()
    res_done = exchange("x", 3, part_of(a_z, own_rows), lambda index, d: res_recv.at[index])
    res_recv[mx] = a_z[pl.ds(pl.multiple_of(mx * own_rows, own_rows), own_rows), :]

    flags_z()
    bias_row, bias_from = iota((ny * 16, 16), 0), iota((ny * 16, 16), 1)
    unpack = jnp.where(
        (bias_row % 16 < images) & (bias_from == (bias_row // 16) * images + bias_row % 16), 1.0, 0.0
    ).astype(BF16)
    for zs in range(nz):
        part = matmul(unpack, f_z[zs]).astype(BF16)
        for ys in range(ny):
            kb[:, (zs * ny + ys) * TILE : (zs * ny + ys + 1) * TILE] = part[ys * 16 : (ys + 1) * 16]
    every_flag = jnp.concatenate([f_z[zs] for zs in range(nz)], axis=0)
    slot_row, slot_from = iota((TILE, nz * 16), 0), iota((TILE, nz * 16), 1)
    source_row = slot_row // cap
    here_lane = iota((TILE, TILE), 1) == seq * cap + iota((TILE, TILE), 0) % cap
    presents = []
    for i in range(images):
        choose = jnp.where(slot_from == (source_row // ny) * 16 + (source_row % ny) * images + i, 1.0, 0.0)
        seen = jnp.where(here_lane, matmul(choose.astype(BF16), every_flag), 0.0)
        presents.append(jnp.where(jnp.sum(seen, axis=1, keepdims=True) < -1.0, 1.0, 0.0))
    taken_ref[...] = jnp.concatenate([jnp.broadcast_to(one, (TILE, TILE)) for one in presents], axis=1)
    q_second()
    lane = iota((TILE, cols), 1)
    head_masks = [jnp.where(lane // HD == h, 1.0, 0.0) for h in range(cols // HD)]
    heads = len(head_masks)
    found_q = q_z[...]
    block = math.gcd(2048, tiles * TILE)
    lookups = []
    stacked = []
    for i in range(images):
        here = jnp.where(presents[i] > 0, found_q[:, i * cols : (i + 1) * cols].astype(F32), mask_query)
        stacked.append(jnp.concatenate([here * one for one in head_masks], axis=0).astype(BF16))

    def fold(state, scores, values_of):
        top, total, accum = state
        new_top = jnp.maximum(top, jnp.max(scores, axis=1, keepdims=True))
        fix = jnp.exp2(top - new_top)
        expo = jnp.exp2(scores - new_top)
        total = total * fix + jnp.sum(expo, axis=1, keepdims=True)
        accum = accum * fix + values_of(expo.astype(BF16))
        return new_top, total, accum

    for i in range(images):
        select = jnp.where(iota((heads * TILE, 16), 1) == i, 1.0, 0.0).astype(BF16)
        lookups.append(jnp.concatenate([stacked[i], select], axis=1))

    def masked_block(number, states):
        where = slice(number * block, (number + 1) * block)
        keys = jnp.concatenate([kt[:, where], kb[:, where]], axis=0)
        scores = [matmul(one, keys) for one in lookups]
        return tuple(
            fold(state, one, lambda expo: contract_last(expo, vt[:, where])) for state, one in zip(states, scores)
        )

    start = (
        jnp.full((heads * TILE, 1), BIG, F32),
        jnp.zeros((heads * TILE, 1), F32),
        jnp.zeros((heads * TILE, cols), F32),
    )
    states = (start,) * images
    for number in range(tiles * TILE // block):
        states = masked_block(number, states)

    lookups = [jnp.concatenate([jnp.zeros_like(one), one], axis=1) for one in stacked]

    def visible(states, first, last):
        spans = [slice(first * sizes[axes[i][0]] * vis, last * sizes[axes[i][0]] * vis) for i in range(images)]
        scores = [contract_last(lookups[i], kv[i, spans[i], :]) for i in range(images)]
        return [
            fold(states[i], scores[i], lambda expo, i=i: matmul(expo, kv[i, spans[i], :])[:, :cols])
            for i in range(images)
        ]

    near = 5 if nz == 8 else 1
    for first, last in ((0, near), (near, nz)):
        for i in range(images):
            for second in seconds[i]:
                second(near_first(sizes[axes[i][1]])[max(first, 1) : last])
        states = visible(states, first, last)
    gathered = []
    for i in range(images):
        top, total, accum = states[i]
        accum = accum / total
        attended = jnp.zeros((TILE, cols), F32)
        for h in range(heads):
            attended = attended + accum[h * TILE : (h + 1) * TILE] * head_masks[h]
        gathered.append(attended)
    att_send[...] = jnp.concatenate(gathered, axis=1).astype(BF16)
    sent = len(pending)
    att_done = exchange("x", 5, part_of(att_send, own_rows), lambda index, d: att_recv.at[index])
    tile_mine = pl.ds(pl.multiple_of(mx * own_rows, own_rows), own_rows)
    att_recv[mx] = att_send[tile_mine, :]

    res_done()
    my_pos = tile_pos[tile_mine, :]
    chunk = width // nx
    bases = []
    for i in range(images):
        rows_here = jnp.concatenate(
            [res_recv[j, :, i * chunk : (i + 1) * chunk] for j in range(nx)], axis=1
        ).astype(F32)
        present = taken_ref[tile_mine, i * TILE : i * TILE + 1]
        bases.append(jnp.where(present > 0, rows_here, mask) + my_pos)
    for copy in pending[:sent]:
        copy.wait_send()
    wp_done()
    att_done()
    sums = jnp.concatenate(bases, axis=0)
    for j in range(nx):
        pieces = [att_recv[j, :, i * cols : (i + 1) * cols] for i in range(images)]
        sums = sums + matmul(jnp.concatenate(pieces, axis=0), wp_all[j])
    for i in range(images):
        out_ref[i] = sums[i * own_rows : (i + 1) * own_rows].astype(BF16)
    for copy in pending[sent:]:
        copy.wait_send()


def local(
    enc_tokens,
    enc_gain,
    enc_bias,
    w_in,
    w_out,
    final_gain,
    w_embed,
    dest,
    mask_token,
    dec_gain,
    w_query,
    w_key,
    w_value,
    w_proj,
):
    images, vis, model_width = enc_tokens.shape
    seq_count = lax.axis_size("seq")
    nx = lax.axis_size("mp")
    ny = math.isqrt(seq_count)
    nz = seq_count // ny
    width = mask_token.shape[0]
    cols = w_query.shape[1]
    cap = TILE // seq_count
    rows = images * vis
    own = TILE // nx
    patches = seq_count * TILE

    low = min(4, seq_count // 2)
    s_low, t, c = np.meshgrid(np.arange(low), np.arange(seq_count), np.arange(cap), indexing="ij")
    place = (s_low * cap + t * TILE + c).reshape(-1)
    wave_t = waves(int(place.max()) + 1, 1, width)[place].T.astype(jnp.bfloat16)
    near = waves(TILE, 1, width)
    far = waves(seq_count, TILE, width)
    rot = waves(seq_count // low, low * cap, width)
    zi, yi, ci = np.meshgrid(np.arange(nz), np.arange(ny), np.arange(cap), indexing="ij")
    perm = np.zeros((TILE, TILE), np.float32)
    perm[np.arange(TILE), ((yi * nz + zi) * cap + ci).reshape(-1)] = 1.0

    hbm = pl.BlockSpec(memory_space=pltpu.HBM)
    vmem = pl.BlockSpec(memory_space=pltpu.VMEM)
    operands = (
        enc_tokens.reshape(rows, model_width),
        enc_gain,
        enc_bias,
        w_in,
        w_out,
        w_proj,
        dest.transpose(0, 2, 1),
        jnp.asarray(far),
        jnp.asarray(near),
        mask_token,
        dec_gain,
        w_key.T,
        w_value.T,
        jnp.asarray(wave_t),
        jnp.asarray(rot),
        final_gain,
        w_embed,
        jnp.asarray(perm, BF16),
        w_query.T,
    )
    block_rows = rows // nx
    dma = pltpu.SemaphoreType.DMA
    scratch = [
        *[pltpu.VMEM(operand.shape, operand.dtype) for operand in operands],
        pltpu.VMEM((rows, model_width), F32),
        pltpu.VMEM((rows, model_width), BF16),
        pltpu.VMEM((nx - 1, block_rows, model_width), BF16),
        pltpu.VMEM((rows, model_width), BF16),
        pltpu.VMEM((nx, rows, width // nx), BF16),
        *[pltpu.VMEM((TILE, images * width // nx), BF16)] * 4,
        *[pltpu.VMEM((TILE, images * cols), BF16)] * 4,
        pltpu.VMEM((images, seq_count * vis, 2 * cols), BF16),
        pltpu.VMEM((cols, patches), BF16),
        pltpu.VMEM((16, patches), BF16),
        pltpu.VMEM((cols, patches), BF16),
        pltpu.VMEM((nx, own, images * width // nx), BF16),
        pltpu.VMEM((TILE, width), F32),
        pltpu.VMEM((2 * cols + 16, width), F32),
        pltpu.VMEM((ny, 16, TILE), BF16),
        pltpu.VMEM((nz, 16, TILE), BF16),
        pltpu.VMEM((TILE, images * TILE), F32),
        pltpu.VMEM((nx, cols, width), BF16),
        pltpu.VMEM((TILE, images * cols), BF16),
        pltpu.VMEM((nx, own, images * cols), BF16),
        dma((len(operands),)),
        dma((6, nx - 1)),
        dma((6, nx - 1)),
        dma((8, ny - 1)),
        dma((8, ny - 1)),
        dma((8, nz - 1)),
        dma((8, nz - 1)),
    ]
    return pl.pallas_call(
        functools.partial(kernel, (nx, ny, nz, images, vis)),
        out_shape=pltpu.VMEM((images, own, width), BF16),
        in_specs=[hbm] * len(operands),
        out_specs=vmem,
        scratch_shapes=scratch,
        compiler_params=pltpu.CompilerParams(
            collective_id=0, has_side_effects=True, vmem_limit_bytes=63300000
        ),
    )(*operands)


def solution(mesh):
    placed = (
        P("dp", "seq", None),
        P(),
        P(),
        P(None, "mp"),
        P("mp", None),
        P(),
        P(None, "mp"),
        P("dp", "seq", None),
        P(),
        P(),
        P(None, "mp"),
        P(None, "mp"),
        P(None, "mp"),
        P("mp", None),
    )
    return jax.shard_map(
        local, mesh=mesh, in_specs=placed, out_specs=P("dp", ("seq", "mp"), None), check_vma=False
    )
```

```python
import functools
import math

import jax
import jax.numpy as jnp
import numpy as np
from jax import lax
from jax.experimental import pallas as pl
from jax.experimental.pallas import tpu as pltpu
from jax.sharding import PartitionSpec as P

HD = 32
TILE = 128
BIG = -1e30
MESH = pl.DeviceIdType.MESH
F32 = jnp.float32
BF16 = jnp.bfloat16


def contract_last(left, right):
    return lax.dot_general(left, right, (((1,), (1,)), ((), ())), preferred_element_type=F32)


def matmul(left, right):
    return jnp.dot(left, right, preferred_element_type=F32)


def normalize(values):
    average = jnp.mean(values, axis=-1, keepdims=True)
    centered = values - average
    spread = jnp.mean(centered * centered, axis=-1, keepdims=True)
    return centered * lax.rsqrt(spread + 1e-06)


def iota(shape, dim):
    return lax.broadcasted_iota(jnp.int32, shape, dim)


def waves(count, scale, width):
    half = width // 2
    freqs = 1.0 / 10000.0 ** (np.arange(half, dtype=np.float64) / half)
    angle = (np.arange(count, dtype=np.float64) * scale)[:, None] * freqs[None, :]
    return np.concatenate([np.sin(angle), np.cos(angle)], axis=-1).astype(np.float32)


def turned(first, second):
    half = first.shape[-1] // 2
    sin_a, cos_a = first[:, :half], first[:, half:]
    sin_b, cos_b = second[:, :half], second[:, half:]
    return jnp.concatenate([sin_a * cos_b + cos_a * sin_b, cos_a * cos_b - sin_a * sin_b], axis=-1)


def picked(one_hot, table):
    high = table.astype(BF16)
    low = (table - high.astype(F32)).astype(BF16)
    return matmul(one_hot, high) + matmul(one_hot, low)


def kernel(
    cfg,
    *refs,
):
    inputs, out_ref, held = refs[:19], refs[19], refs[20:39]
    (
        part_own,
        part_send,
        rs_recv,
        enc_all,
        e_all,
        a_src,
        a_y,
        a_mid,
        a_z,
        q_src,
        q_y,
        q_mid,
        q_z,
        kv,
        kt,
        kb,
        vt,
        res_recv,
        tile_pos,
        stat_w,
        f_y,
        f_z,
        taken_ref,
        wp_all,
        att_send,
        att_recv,
        local_sem,
        x_send,
        x_recv,
        y_send,
        y_recv,
        z_send,
        z_recv,
    ) = refs[39:]
    (
        tok_ref,
        gain_ref,
        bias_ref,
        w_in,
        w_out,
        w_proj_ref,
        dest_ref,
        far_ref,
        near_ref,
        mask_ref,
        dec_gain_ref,
        wk_ref,
        wv_ref,
        wave_t,
        rot_ref,
        final_ref,
        w_embed,
        perm_ref,
        wq_ref,
    ) = held
    nx, ny, nz, images, vis = cfg
    tiles = ny * nz
    cap = TILE // tiles
    rows = images * vis
    block_rows = rows // nx
    width = out_ref.shape[2]
    cols = wq_ref.shape[0]
    own_rows = TILE // nx
    seq = lax.axis_index("seq")
    mx = lax.axis_index("mp")
    z, y = seq // ny, seq % ny

    loads = []
    for number, (src, dst) in enumerate(zip(inputs, held)):
        loads.append(pltpu.make_async_copy(src, dst, local_sem.at[number]))

    def load_now(first, last):
        for load in loads[first:last]:
            load.start()

    load_now(0, 5)

    def loaded(first, last):
        for load in loads[first:last]:
            load.wait()

    def partner(axis, d):
        if axis == "x":
            index = lax.rem(mx + d, nx)
            return index, {"mp": index}
        if axis == "y":
            index = lax.rem(y + d, ny)
            return index, {"seq": z * ny + index}
        index = lax.rem(z + d, nz)
        return index, {"seq": index * ny + y}

    sizes = {"x": nx, "y": ny, "z": nz}
    places = {"x": mx, "y": y, "z": z}
    sems = {"x": (x_send, x_recv), "y": (y_send, y_recv), "z": (z_send, z_recv)}
    barrier = pltpu.get_barrier_semaphore()
    for axis in "xyz":
        for d in range(1, sizes[axis]):
            pl.semaphore_signal(barrier, inc=1, device_id=partner(axis, d)[1], device_id_type=MESH)

    pending = []

    def near_first(size):
        return sorted(range(size), key=lambda d: (min(d, size - d), d))

    def exchange(axis, group, source, target, steps=None):
        size = sizes[axis]
        send, recv = sems[axis]
        steps = near_first(size)[1:] if steps is None else steps
        open_steps = list(steps)
        for d in steps[::-1]:
            index, device = partner(axis, d)
            copy = pltpu.make_async_remote_copy(
                src_ref=source(index),
                dst_ref=target(places[axis], d),
                send_sem=send.at[group, d - 1],
                recv_sem=recv.at[group, d - 1],
                device_id=device,
                device_id_type=MESH,
            )
            copy.start()
            pending.append(copy)

        def arrived(wanted=steps):
            for d in [d for d in wanted if d in open_steps]:
                open_steps.remove(d)
                sender, device = partner(axis, size - d)
                pltpu.make_async_remote_copy(
                    src_ref=target(sender, d),
                    dst_ref=target(sender, d),
                    send_sem=send.at[group, d - 1],
                    recv_sem=recv.at[group, d - 1],
                    device_id=device,
                    device_id_type=MESH,
                ).wait_recv()

        return arrived

    def part_of(ref, count):
        return lambda index, d=0: ref.at[pl.ds(pl.multiple_of(index * count, count), count)]

    load_now(5, len(loads))
    loaded(0, 3)
    tokens = tok_ref[...].astype(F32)
    normed = (normalize(tokens) * gain_ref[...][None, :] + bias_ref[...][None, :]).astype(BF16)
    loaded(3, 4)
    pre = matmul(normed, w_in[...])
    hidden = (0.5 * pre * (1.0 + lax.erf(pre * math.sqrt(0.5)))).astype(BF16)
    loaded(4, 5)
    partial = matmul(hidden, w_out[...])
    part_own[...] = partial
    part_send[...] = partial.astype(BF16)
    pl.semaphore_wait(barrier, (nx - 1) + (ny - 1) + (nz - 1))
    rs_done = exchange("x", 0, part_of(part_send, block_rows), lambda index, d: rs_recv.at[d - 1])
    loaded(5, 6)
    wp_all[mx] = w_proj_ref[...]
    wp_done = exchange("x", 4, lambda index: wp_all.at[mx], lambda index, d: wp_all.at[index])

    loaded(6, 15)
    dest_row = jnp.concatenate([dest_ref[i] for i in range(images)], axis=1)
    eye = iota((rows, rows), 0) == iota((rows, rows), 1)
    dest_col = jnp.sum(jnp.where(eye, dest_row, 0), axis=1, keepdims=True)
    same = (dest_col == dest_row) & (iota((rows, rows), 0) // vis == iota((rows, rows), 1) // vis)
    rank_col = jnp.sum(
        jnp.where(same & (iota((rows, rows), 1) < iota((rows, rows), 0)), 1, 0), axis=1, keepdims=True
    )
    rank_row = jnp.sum(
        jnp.where(same & (iota((rows, rows), 0) < iota((rows, rows), 1)), 1, 0), axis=0, keepdims=True
    )
    slot_col = dest_col * cap + rank_col
    hits = jnp.where(slot_col == iota((rows, TILE), 1), 1.0, 0.0)
    flag_rows = jnp.zeros((16, TILE), F32)
    for i in range(images):
        count = jnp.sum(hits[i * vis : (i + 1) * vis], axis=0, keepdims=True)
        flag_rows = jnp.where(iota((16, TILE), 0) == i, count, flag_rows)

    f_y[y] = (flag_rows * BIG).astype(BF16)
    flags_y = exchange("y", 0, lambda index: f_y.at[y], lambda index, d: f_y.at[index])
    order_row = ((dest_row % ny) * nz + dest_row // ny) * cap + rank_row
    spread_f = jnp.where(order_row == iota((TILE, rows), 0), 1.0, 0.0)
    lane_image = iota((TILE, rows), 1) // vis
    spreads = [jnp.where(lane_image == i, spread_f, 0.0) for i in range(images)]
    spreads = [one.astype(BF16) for one in spreads]

    at_tile = jnp.where(dest_col == iota((rows, tiles), 1), 1.0, 0.0).astype(BF16)
    at_place = jnp.where(seq * cap + rank_col == iota((rows, TILE), 1), 1.0, 0.0).astype(BF16)
    vis_pos = turned(picked(at_tile, far_ref[...]), picked(at_place, near_ref[...]))
    tile_pos[...] = turned(near_ref[...], far_ref[pl.ds(seq, 1), :])

    mask = mask_ref[...].astype(F32)[None, :]
    dec_gain = dec_gain_ref[...][None, :]
    mask_mid = mask - jnp.mean(mask, axis=-1, keepdims=True)
    mask_spread = jnp.mean(mask_mid * mask_mid, axis=-1, keepdims=True) + 0.5
    kv_cols = 2 * cols
    gained = jnp.concatenate([wk_ref[...], wv_ref[...]], axis=0).astype(F32) * dec_gain
    stat_w[0:kv_cols, :] = gained
    gain_sum = jnp.sum(gained, axis=1, keepdims=True)
    mask_sum = jnp.sum(gained * mask_mid, axis=1, keepdims=True)
    stat_rows = iota((16, width), 0)
    stat_w[kv_cols:, :] = jnp.where(stat_rows == 0, 1.0, jnp.where(stat_rows == 1, mask_mid, 0.0)) * (1.0 / width)
    lanes = wave_t.shape[1]
    half = width // 2

    def table_step(step, carry):
        turn = rot_ref[pl.ds(step, 1), :]
        sin_t, cos_t = turn[:, :half], turn[:, half:]
        sin_w, cos_w = stat_w[:, :half], stat_w[:, half:]
        rotated = jnp.concatenate(
            [(sin_w * cos_t - cos_w * sin_t).astype(BF16), (sin_w * sin_t + cos_w * cos_t).astype(BF16)], axis=1
        )
        found = matmul(rotated, wave_t[...])
        average = found[kv_cols : kv_cols + 1]
        spread = mask_spread + 2.0 * found[kv_cols + 1 : kv_cols + 2] - average * average
        scale = lax.rsqrt(jnp.maximum(spread, 0.0) + 1e-06)
        made = ((found[:kv_cols] + mask_sum - average * gain_sum) * scale).astype(BF16)
        where = pl.ds(pl.multiple_of(step * lanes, lanes), lanes)
        kt[:, where] = made[:cols]
        vt[:, where] = made[cols:]
        return carry

    steps = rot_ref.shape[0]
    cut = [0, steps * 3 // 8, steps * 6 // 8, steps]
    lax.fori_loop(cut[0], cut[1], table_step, 0)

    loaded(15, 19)
    rs_done()
    mine = pl.ds(pl.multiple_of(mx * block_rows, block_rows), block_rows)
    mixed = tok_ref[mine, :].astype(F32) + part_own[mine, :]
    for d in range(nx - 1):
        mixed = mixed + rs_recv[d].astype(F32)
    enc_all[mine, :] = (normalize(mixed) * final_ref[...][None, :]).astype(BF16)
    enc_done = exchange(
        "x", 1, lambda index: part_of(enc_all, block_rows)(mx), lambda index, d: part_of(enc_all, block_rows)(index)
    )
    lax.fori_loop(cut[1], cut[2], table_step, 0)
    flags_y()
    joined = [f_y[i].astype(F32)[:images] for i in range(ny)]
    if ny * images < 16:
        joined.append(jnp.zeros((16 - ny * images, TILE), F32))
    f_z[z] = jnp.concatenate(joined, axis=0).astype(BF16)
    flags_z = exchange("z", 0, lambda index: f_z.at[z], lambda index, d: f_z.at[index])
    enc_done()
    embedded = matmul(enc_all[...], w_embed[...]).astype(BF16)
    e_all[mx] = embedded
    e_done = exchange("x", 2, lambda index: e_all.at[mx], lambda index, d: e_all.at[index])
    ry, rz = nz * cap, ny * cap
    a_src[...] = jnp.concatenate([matmul(one, embedded) for one in spreads], axis=1).astype(BF16)

    def first_leg(group, src, mid):
        done = exchange("y", group, part_of(src, ry), part_of(mid, ry))
        mid[pl.ds(pl.multiple_of(y * ry, ry), ry), :] = src[pl.ds(pl.multiple_of(y * ry, ry), ry), :]
        return done

    def second_leg(group, mid, turned_ref, final):
        turned_ref[...] = matmul(perm_ref[...], mid[...]).astype(BF16)
        done = exchange("z", group, part_of(turned_ref, rz), part_of(final, rz))
        final[pl.ds(pl.multiple_of(z * rz, rz), rz), :] = turned_ref[pl.ds(pl.multiple_of(z * rz, rz), rz), :]
        return done

    a_first = first_leg(1, a_src, a_y)
    lax.fori_loop(cut[2], cut[3], table_step, 0)

    score_scale = math.log2(math.e) / math.sqrt(HD)
    mask_rows = (normalize(mask + tile_pos[...]) * dec_gain).astype(BF16)
    mask_query = contract_last(mask_rows, wq_ref[...]) * score_scale

    e_done()
    full = jnp.concatenate([e_all[i] for i in range(nx)], axis=1).astype(F32)
    vis_rows = (normalize(full + vis_pos) * dec_gain).astype(BF16)
    query = (contract_last(vis_rows, wq_ref[...]) * score_scale).astype(BF16)
    q_src[...] = jnp.concatenate([matmul(one, query) for one in spreads], axis=1).astype(BF16)
    q_first = first_leg(2, q_src, q_y)
    vis_kv = contract_last(vis_rows, jnp.concatenate([wv_ref[...], wk_ref[...]], axis=0)).astype(BF16)
    for i in range(images):
        kv[i, :vis, :] = vis_kv[i * vis : (i + 1) * vis]
    axes = [("y", "z"), ("z", "y")]
    firsts, seconds = [], [[] for _ in range(images)]

    def slots(i, first, last, outer=0):
        lead = outer * sizes[axes[i][0]]
        return kv.at[i, (lead + first) * vis : (lead + last) * vis]

    def place_of(axis, d):
        return near_first(sizes[axis]).index(d)

    for i in range(images):
        one, two = axes[i]
        firsts.append(
            exchange(
                one,
                3,
                lambda index, i=i: slots(i, 0, 1),
                lambda index, d, i=i, one=one: slots(i, place_of(one, d), place_of(one, d) + 1),
            )
        )

    def forward(i, group, first, last, steps=None):
        two = axes[i][1]
        seconds[i].append(
            exchange(
                two,
                group,
                lambda index: slots(i, first, last),
                lambda index, d: slots(i, first, last, place_of(two, d)),
                steps,
            )
        )

    def relay(i, group, first, last, carried):
        two = axes[i][1]
        send, recv = sems[two]
        copies = {}
        for second in carried:
            second([2, 6])
        for total, via in ((4, 2), (3, 2), (5, 6)):
            copies[total] = pltpu.make_async_remote_copy(
                src_ref=slots(i, first, last, place_of(two, via)),
                dst_ref=slots(i, first, last, place_of(two, total)),
                send_sem=send.at[group, total - 1],
                recv_sem=recv.at[group, total - 1],
                device_id=partner(two, (total - via) % sizes[two])[1],
                device_id_type=MESH,
            )
            copies[total].start()
            pending.append(copies[total])

        def arrived(wanted):
            for d in [d for d in wanted if d in copies]:
                back = partner(two, sizes[two] - d)[1]
                pltpu.make_async_remote_copy(
                    src_ref=slots(i, first, last, place_of(two, d)),
                    dst_ref=slots(i, first, last, place_of(two, d)),
                    send_sem=send.at[group, d - 1],
                    recv_sem=recv.at[group, d - 1],
                    device_id=back,
                    device_id_type=MESH,
                ).wait_recv()
                del copies[d]

        return arrived

    relayed = ny == 8 and nz == 8
    close = [1, 7, 2, 6] if relayed else None
    relays = [[] for _ in range(images)]

    def cuts(size):
        return [(1, 3), (3, 5), (5, 8)] if size == 8 else [(1, size)]

    a_first()
    a_second = second_leg(1, a_y, a_mid, a_z)
    for i in range(images):
        forward(i, 4, 0, 1, close)
    for number in range(len(cuts(ny))):
        for i in range(images)[::-1]:
            if number == 0 and i == 0:
                q_first()
                q_second = second_leg(2, q_y, q_mid, q_z)
            size = sizes[axes[i][0]]
            first, last = cuts(size)[number]
            firsts[i](near_first(size)[first:last])
            forward(i, 5 + number, first, last, close if number < 2 else None)
    a_second()
    res_done = exchange("x", 3, part_of(a_z, own_rows), lambda index, d: res_recv.at[index])
    res_recv[mx] = a_z[pl.ds(pl.multiple_of(mx * own_rows, own_rows), own_rows), :]

    flags_z()
    bias_row, bias_from = iota((ny * 16, 16), 0), iota((ny * 16, 16), 1)
    unpack = jnp.where(
        (bias_row % 16 < images) & (bias_from == (bias_row // 16) * images + bias_row % 16), 1.0, 0.0
    ).astype(BF16)
    for zs in range(nz):
        part = matmul(unpack, f_z[zs]).astype(BF16)
        for ys in range(ny):
            kb[:, (zs * ny + ys) * TILE : (zs * ny + ys + 1) * TILE] = part[ys * 16 : (ys + 1) * 16]
    every_flag = jnp.concatenate([f_z[zs] for zs in range(nz)], axis=0)
    slot_row, slot_from = iota((TILE, nz * 16), 0), iota((TILE, nz * 16), 1)
    source_row = slot_row // cap
    here_lane = iota((TILE, TILE), 1) == seq * cap + iota((TILE, TILE), 0) % cap
    presents = []
    for i in range(images):
        choose = jnp.where(slot_from == (source_row // ny) * 16 + (source_row % ny) * images + i, 1.0, 0.0)
        seen = jnp.where(here_lane, matmul(choose.astype(BF16), every_flag), 0.0)
        presents.append(jnp.where(jnp.sum(seen, axis=1, keepdims=True) < -1.0, 1.0, 0.0))
    if relayed:
        for i in range(images)[::-1]:
            relays[i].append(relay(i, 8, 0, 3, seconds[i][:2]))
    taken_ref[...] = jnp.concatenate([jnp.broadcast_to(one, (TILE, TILE)) for one in presents], axis=1)
    q_second()
    lane = iota((TILE, cols), 1)
    head_masks = [jnp.where(lane // HD == h, 1.0, 0.0) for h in range(cols // HD)]
    heads = len(head_masks)
    found_q = q_z[...]
    block = math.gcd(2048, tiles * TILE)
    lookups = []
    stacked = []
    for i in range(images):
        here = jnp.where(presents[i] > 0, found_q[:, i * cols : (i + 1) * cols].astype(F32), mask_query)
        stacked.append(jnp.concatenate([here * one for one in head_masks], axis=0).astype(BF16))

    def fold(state, scores, values_of):
        top, total, accum = state
        new_top = jnp.maximum(top, jnp.max(scores, axis=1, keepdims=True))
        fix = jnp.exp2(top - new_top)
        expo = jnp.exp2(scores - new_top)
        total = total * fix + jnp.sum(expo, axis=1, keepdims=True)
        accum = accum * fix + values_of(expo.astype(BF16))
        return new_top, total, accum

    for i in range(images):
        select = jnp.where(iota((heads * TILE, 16), 1) == i, 1.0, 0.0).astype(BF16)
        lookups.append(jnp.concatenate([stacked[i], select], axis=1))

    def masked_block(number, states):
        where = slice(number * block, (number + 1) * block)
        keys = jnp.concatenate([kt[:, where], kb[:, where]], axis=0)
        scores = [matmul(one, keys) for one in lookups]
        return tuple(
            fold(state, one, lambda expo: contract_last(expo, vt[:, where])) for state, one in zip(states, scores)
        )

    start = (
        jnp.full((heads * TILE, 1), BIG, F32),
        jnp.zeros((heads * TILE, 1), F32),
        jnp.zeros((heads * TILE, cols), F32),
    )
    states = (start,) * images
    for number in range(tiles * TILE // block):
        states = masked_block(number, states)
        if relayed and number == 0:
            for i in range(images)[::-1]:
                relays[i].append(relay(i, 9, 3, 5, seconds[i][2:3]))

    lookups = [jnp.concatenate([jnp.zeros_like(one), one], axis=1) for one in stacked]

    def visible(states, first, last):
        spans = [slice(first * sizes[axes[i][0]] * vis, last * sizes[axes[i][0]] * vis) for i in range(images)]
        scores = [contract_last(lookups[i], kv[i, spans[i], :]) for i in range(images)]
        return [
            fold(states[i], scores[i], lambda expo, i=i: matmul(expo, kv[i, spans[i], :])[:, :cols])
            for i in range(images)
        ]

    near = 5 if nz == 8 else 1
    for first, last in ((0, near), (near, nz)):
        for i in range(images):
            for second in seconds[i] + relays[i]:
                second(near_first(sizes[axes[i][1]])[max(first, 1) : last])
        states = visible(states, first, last)
    gathered = []
    for i in range(images):
        top, total, accum = states[i]
        accum = accum / total
        attended = jnp.zeros((TILE, cols), F32)
        for h in range(heads):
            attended = attended + accum[h * TILE : (h + 1) * TILE] * head_masks[h]
        gathered.append(attended)
    att_send[...] = jnp.concatenate(gathered, axis=1).astype(BF16)
    sent = len(pending)
    att_done = exchange("x", 5, part_of(att_send, own_rows), lambda index, d: att_recv.at[index])
    tile_mine = pl.ds(pl.multiple_of(mx * own_rows, own_rows), own_rows)
    att_recv[mx] = att_send[tile_mine, :]

    res_done()
    my_pos = tile_pos[tile_mine, :]
    chunk = width // nx
    bases = []
    for i in range(images):
        rows_here = jnp.concatenate(
            [res_recv[j, :, i * chunk : (i + 1) * chunk] for j in range(nx)], axis=1
        ).astype(F32)
        present = taken_ref[tile_mine, i * TILE : i * TILE + 1]
        bases.append(jnp.where(present > 0, rows_here, mask) + my_pos)
    for copy in pending[:sent]:
        copy.wait_send()
    wp_done()
    att_done()
    sums = jnp.concatenate(bases, axis=0)
    for j in range(nx):
        pieces = [att_recv[j, :, i * cols : (i + 1) * cols] for i in range(images)]
        sums = sums + matmul(jnp.concatenate(pieces, axis=0), wp_all[j])
    for i in range(images):
        out_ref[i] = sums[i * own_rows : (i + 1) * own_rows].astype(BF16)
    for copy in pending[sent:]:
        copy.wait_send()


def local(
    enc_tokens,
    enc_gain,
    enc_bias,
    w_in,
    w_out,
    final_gain,
    w_embed,
    dest,
    mask_token,
    dec_gain,
    w_query,
    w_key,
    w_value,
    w_proj,
):
    images, vis, model_width = enc_tokens.shape
    seq_count = lax.axis_size("seq")
    nx = lax.axis_size("mp")
    ny = math.isqrt(seq_count)
    nz = seq_count // ny
    width = mask_token.shape[0]
    cols = w_query.shape[1]
    cap = TILE // seq_count
    rows = images * vis
    own = TILE // nx
    patches = seq_count * TILE

    low = min(4, seq_count // 2)
    s_low, t, c = np.meshgrid(np.arange(low), np.arange(seq_count), np.arange(cap), indexing="ij")
    place = (s_low * cap + t * TILE + c).reshape(-1)
    wave_t = waves(int(place.max()) + 1, 1, width)[place].T.astype(jnp.bfloat16)
    near = waves(TILE, 1, width)
    far = waves(seq_count, TILE, width)
    rot = waves(seq_count // low, low * cap, width)
    zi, yi, ci = np.meshgrid(np.arange(nz), np.arange(ny), np.arange(cap), indexing="ij")
    perm = np.zeros((TILE, TILE), np.float32)
    perm[np.arange(TILE), ((yi * nz + zi) * cap + ci).reshape(-1)] = 1.0

    hbm = pl.BlockSpec(memory_space=pltpu.HBM)
    vmem = pl.BlockSpec(memory_space=pltpu.VMEM)
    operands = (
        enc_tokens.reshape(rows, model_width),
        enc_gain,
        enc_bias,
        w_in,
        w_out,
        w_proj,
        dest.transpose(0, 2, 1),
        jnp.asarray(far),
        jnp.asarray(near),
        mask_token,
        dec_gain,
        w_key.T,
        w_value.T,
        jnp.asarray(wave_t),
        jnp.asarray(rot),
        final_gain,
        w_embed,
        jnp.asarray(perm, BF16),
        w_query.T,
    )
    block_rows = rows // nx
    dma = pltpu.SemaphoreType.DMA
    scratch = [
        *[pltpu.VMEM(operand.shape, operand.dtype) for operand in operands],
        pltpu.VMEM((rows, model_width), F32),
        pltpu.VMEM((rows, model_width), BF16),
        pltpu.VMEM((nx - 1, block_rows, model_width), BF16),
        pltpu.VMEM((rows, model_width), BF16),
        pltpu.VMEM((nx, rows, width // nx), BF16),
        *[pltpu.VMEM((TILE, images * width // nx), BF16)] * 4,
        *[pltpu.VMEM((TILE, images * cols), BF16)] * 4,
        pltpu.VMEM((images, seq_count * vis, 2 * cols), BF16),
        pltpu.VMEM((cols, patches), BF16),
        pltpu.VMEM((16, patches), BF16),
        pltpu.VMEM((cols, patches), BF16),
        pltpu.VMEM((nx, own, images * width // nx), BF16),
        pltpu.VMEM((TILE, width), F32),
        pltpu.VMEM((2 * cols + 16, width), F32),
        pltpu.VMEM((ny, 16, TILE), BF16),
        pltpu.VMEM((nz, 16, TILE), BF16),
        pltpu.VMEM((TILE, images * TILE), F32),
        pltpu.VMEM((nx, cols, width), BF16),
        pltpu.VMEM((TILE, images * cols), BF16),
        pltpu.VMEM((nx, own, images * cols), BF16),
        dma((len(operands),)),
        dma((6, nx - 1)),
        dma((6, nx - 1)),
        dma((10, ny - 1)),
        dma((10, ny - 1)),
        dma((10, nz - 1)),
        dma((10, nz - 1)),
    ]
    return pl.pallas_call(
        functools.partial(kernel, (nx, ny, nz, images, vis)),
        out_shape=pltpu.VMEM((images, own, width), BF16),
        in_specs=[hbm] * len(operands),
        out_specs=vmem,
        scratch_shapes=scratch,
        compiler_params=pltpu.CompilerParams(
            collective_id=0, has_side_effects=True, vmem_limit_bytes=63300000
        ),
    )(*operands)


def solution(mesh):
    placed = (
        P("dp", "seq", None),
        P(),
        P(),
        P(None, "mp"),
        P("mp", None),
        P(),
        P(None, "mp"),
        P("dp", "seq", None),
        P(),
        P(),
        P(None, "mp"),
        P(None, "mp"),
        P(None, "mp"),
        P("mp", None),
    )
    return jax.shard_map(
        local, mesh=mesh, in_specs=placed, out_specs=P("dp", ("seq", "mp"), None), check_vma=False
    )
```

```python
import functools
import math

import jax
import jax.numpy as jnp
import numpy as np
from jax import lax
from jax.experimental import pallas as pl
from jax.experimental.pallas import tpu as pltpu
from jax.sharding import PartitionSpec as P

HD = 32
TILE = 128
BIG = -1e30
MESH = pl.DeviceIdType.MESH
F32 = jnp.float32
BF16 = jnp.bfloat16


def contract_last(left, right):
    return lax.dot_general(left, right, (((1,), (1,)), ((), ())), preferred_element_type=F32)


def matmul(left, right):
    return jnp.dot(left, right, preferred_element_type=F32)


def normalize(values):
    average = jnp.mean(values, axis=-1, keepdims=True)
    centered = values - average
    spread = jnp.mean(centered * centered, axis=-1, keepdims=True)
    return centered * lax.rsqrt(spread + 1e-06)


def iota(shape, dim):
    return lax.broadcasted_iota(jnp.int32, shape, dim)


def waves(count, scale, width):
    half = width // 2
    freqs = 1.0 / 10000.0 ** (np.arange(half, dtype=np.float64) / half)
    angle = (np.arange(count, dtype=np.float64) * scale)[:, None] * freqs[None, :]
    return np.concatenate([np.sin(angle), np.cos(angle)], axis=-1).astype(np.float32)


def turned(first, second):
    half = first.shape[-1] // 2
    sin_a, cos_a = first[:, :half], first[:, half:]
    sin_b, cos_b = second[:, :half], second[:, half:]
    return jnp.concatenate([sin_a * cos_b + cos_a * sin_b, cos_a * cos_b - sin_a * sin_b], axis=-1)


def picked(one_hot, table):
    high = table.astype(BF16)
    low = (table - high.astype(F32)).astype(BF16)
    return matmul(one_hot, high) + matmul(one_hot, low)


def kernel(
    cfg,
    *refs,
):
    inputs, out_ref, held = refs[:19], refs[19], refs[20:39]
    (
        part_own,
        part_send,
        rs_recv,
        enc_all,
        e_all,
        a_src,
        a_y,
        a_mid,
        a_z,
        q_src,
        q_y,
        q_mid,
        q_z,
        kv,
        kt,
        kb,
        vt,
        res_recv,
        tile_pos,
        stat_w,
        f_y,
        f_z,
        taken_ref,
        wp_all,
        att_send,
        att_recv,
        local_sem,
        x_send,
        x_recv,
        y_send,
        y_recv,
        z_send,
        z_recv,
    ) = refs[39:]
    (
        tok_ref,
        gain_ref,
        bias_ref,
        w_in,
        w_out,
        w_proj_ref,
        dest_ref,
        far_ref,
        near_ref,
        mask_ref,
        dec_gain_ref,
        wk_ref,
        wv_ref,
        wave_t,
        rot_ref,
        final_ref,
        w_embed,
        perm_ref,
        wq_ref,
    ) = held
    nx, ny, nz, images, vis = cfg
    tiles = ny * nz
    cap = TILE // tiles
    rows = images * vis
    block_rows = rows // nx
    width = out_ref.shape[2]
    cols = wq_ref.shape[0]
    own_rows = TILE // nx
    seq = lax.axis_index("seq")
    mx = lax.axis_index("mp")
    z, y = seq // ny, seq % ny

    loads = []
    for number, (src, dst) in enumerate(zip(inputs, held)):
        loads.append(pltpu.make_async_copy(src, dst, local_sem.at[number]))

    def load_now(first, last):
        for load in loads[first:last]:
            load.start()

    load_now(0, 5)

    def loaded(first, last):
        for load in loads[first:last]:
            load.wait()

    def partner(axis, d):
        if axis == "x":
            index = lax.rem(mx + d, nx)
            return index, {"mp": index}
        if axis == "y":
            index = lax.rem(y + d, ny)
            return index, {"seq": z * ny + index}
        index = lax.rem(z + d, nz)
        return index, {"seq": index * ny + y}

    sizes = {"x": nx, "y": ny, "z": nz}
    places = {"x": mx, "y": y, "z": z}
    sems = {"x": (x_send, x_recv), "y": (y_send, y_recv), "z": (z_send, z_recv)}
    barrier = pltpu.get_barrier_semaphore()
    for axis in "xyz":
        for d in range(1, sizes[axis]):
            pl.semaphore_signal(barrier, inc=1, device_id=partner(axis, d)[1], device_id_type=MESH)

    pending = []

    def near_first(size):
        return sorted(range(size), key=lambda d: (min(d, size - d), d))

    def exchange(axis, group, source, target, steps=None):
        size = sizes[axis]
        send, recv = sems[axis]
        steps = near_first(size)[1:] if steps is None else steps
        open_steps = list(steps)
        for d in steps[::-1]:
            index, device = partner(axis, d)
            copy = pltpu.make_async_remote_copy(
                src_ref=source(index),
                dst_ref=target(places[axis], d),
                send_sem=send.at[group, d - 1],
                recv_sem=recv.at[group, d - 1],
                device_id=device,
                device_id_type=MESH,
            )
            copy.start()
            pending.append(copy)

        def arrived(wanted=steps):
            for d in [d for d in wanted if d in open_steps]:
                open_steps.remove(d)
                sender, device = partner(axis, size - d)
                pltpu.make_async_remote_copy(
                    src_ref=target(sender, d),
                    dst_ref=target(sender, d),
                    send_sem=send.at[group, d - 1],
                    recv_sem=recv.at[group, d - 1],
                    device_id=device,
                    device_id_type=MESH,
                ).wait_recv()

        return arrived

    def part_of(ref, count):
        return lambda index, d=0: ref.at[pl.ds(pl.multiple_of(index * count, count), count)]

    load_now(5, len(loads))
    loaded(0, 3)
    tokens = tok_ref[...].astype(F32)
    normed = (normalize(tokens) * gain_ref[...][None, :] + bias_ref[...][None, :]).astype(BF16)
    loaded(3, 4)
    pre = matmul(normed, w_in[...])
    hidden = (0.5 * pre * (1.0 + lax.erf(pre * math.sqrt(0.5)))).astype(BF16)
    loaded(4, 5)
    partial = matmul(hidden, w_out[...])
    part_own[...] = partial
    part_send[...] = partial.astype(BF16)
    pl.semaphore_wait(barrier, (nx - 1) + (ny - 1) + (nz - 1))
    rs_done = exchange("x", 0, part_of(part_send, block_rows), lambda index, d: rs_recv.at[d - 1])
    loaded(5, 6)
    wp_all[mx] = w_proj_ref[...]
    wp_done = exchange("x", 4, lambda index: wp_all.at[mx], lambda index, d: wp_all.at[index])

    loaded(6, 15)
    dest_row = jnp.concatenate([dest_ref[i] for i in range(images)], axis=1)
    eye = iota((rows, rows), 0) == iota((rows, rows), 1)
    dest_col = jnp.sum(jnp.where(eye, dest_row, 0), axis=1, keepdims=True)
    same = (dest_col == dest_row) & (iota((rows, rows), 0) // vis == iota((rows, rows), 1) // vis)
    rank_col = jnp.sum(
        jnp.where(same & (iota((rows, rows), 1) < iota((rows, rows), 0)), 1, 0), axis=1, keepdims=True
    )
    rank_row = jnp.sum(
        jnp.where(same & (iota((rows, rows), 0) < iota((rows, rows), 1)), 1, 0), axis=0, keepdims=True
    )
    slot_col = dest_col * cap + rank_col
    hits = jnp.where(slot_col == iota((rows, TILE), 1), 1.0, 0.0)
    flag_rows = jnp.zeros((16, TILE), F32)
    for i in range(images):
        count = jnp.sum(hits[i * vis : (i + 1) * vis], axis=0, keepdims=True)
        flag_rows = jnp.where(iota((16, TILE), 0) == i, count, flag_rows)

    f_y[y] = (flag_rows * BIG).astype(BF16)
    flags_y = exchange("y", 0, lambda index: f_y.at[y], lambda index, d: f_y.at[index])
    order_row = ((dest_row % ny) * nz + dest_row // ny) * cap + rank_row
    spread_f = jnp.where(order_row == iota((TILE, rows), 0), 1.0, 0.0)
    lane_image = iota((TILE, rows), 1) // vis
    spreads = [jnp.where(lane_image == i, spread_f, 0.0) for i in range(images)]
    spreads = [one.astype(BF16) for one in spreads]

    at_tile = jnp.where(dest_col == iota((rows, tiles), 1), 1.0, 0.0).astype(BF16)
    at_place = jnp.where(seq * cap + rank_col == iota((rows, TILE), 1), 1.0, 0.0).astype(BF16)
    vis_pos = turned(picked(at_tile, far_ref[...]), picked(at_place, near_ref[...]))
    tile_pos[...] = turned(near_ref[...], far_ref[pl.ds(seq, 1), :])

    mask = mask_ref[...].astype(F32)[None, :]
    dec_gain = dec_gain_ref[...][None, :]
    mask_mid = mask - jnp.mean(mask, axis=-1, keepdims=True)
    mask_spread = jnp.mean(mask_mid * mask_mid, axis=-1, keepdims=True) + 0.5
    kv_cols = 2 * cols
    gained = jnp.concatenate([wk_ref[...], wv_ref[...]], axis=0).astype(F32) * dec_gain
    stat_w[0:kv_cols, :] = gained
    gain_sum = jnp.sum(gained, axis=1, keepdims=True)
    mask_sum = jnp.sum(gained * mask_mid, axis=1, keepdims=True)
    stat_rows = iota((16, width), 0)
    stat_w[kv_cols:, :] = jnp.where(stat_rows == 0, 1.0, jnp.where(stat_rows == 1, mask_mid, 0.0)) * (1.0 / width)
    lanes = wave_t.shape[1]
    half = width // 2

    def table_step(step, carry):
        turn = rot_ref[pl.ds(step, 1), :]
        sin_t, cos_t = turn[:, :half], turn[:, half:]
        sin_w, cos_w = stat_w[:, :half], stat_w[:, half:]
        rotated = jnp.concatenate(
            [(sin_w * cos_t - cos_w * sin_t).astype(BF16), (sin_w * sin_t + cos_w * cos_t).astype(BF16)], axis=1
        )
        found = matmul(rotated, wave_t[...])
        average = found[kv_cols : kv_cols + 1]
        spread = mask_spread + 2.0 * found[kv_cols + 1 : kv_cols + 2] - average * average
        scale = lax.rsqrt(jnp.maximum(spread, 0.0) + 1e-06)
        made = ((found[:kv_cols] + mask_sum - average * gain_sum) * scale).astype(BF16)
        where = pl.ds(pl.multiple_of(step * lanes, lanes), lanes)
        kt[:, where] = made[:cols]
        vt[:, where] = made[cols:]
        return carry

    steps = rot_ref.shape[0]
    cut = [0, steps * 3 // 8, steps * 6 // 8, steps]
    lax.fori_loop(cut[0], cut[1], table_step, 0)

    loaded(15, 19)
    rs_done()
    mine = pl.ds(pl.multiple_of(mx * block_rows, block_rows), block_rows)
    mixed = tok_ref[mine, :].astype(F32) + part_own[mine, :]
    for d in range(nx - 1):
        mixed = mixed + rs_recv[d].astype(F32)
    enc_all[mine, :] = (normalize(mixed) * final_ref[...][None, :]).astype(BF16)
    enc_done = exchange(
        "x", 1, lambda index: part_of(enc_all, block_rows)(mx), lambda index, d: part_of(enc_all, block_rows)(index)
    )
    lax.fori_loop(cut[1], cut[2], table_step, 0)
    flags_y()
    joined = [f_y[i].astype(F32)[:images] for i in range(ny)]
    if ny * images < 16:
        joined.append(jnp.zeros((16 - ny * images, TILE), F32))
    f_z[z] = jnp.concatenate(joined, axis=0).astype(BF16)
    flags_z = exchange("z", 0, lambda index: f_z.at[z], lambda index, d: f_z.at[index])
    enc_done()
    embedded = matmul(enc_all[...], w_embed[...]).astype(BF16)
    e_all[mx] = embedded
    e_done = exchange("x", 2, lambda index: e_all.at[mx], lambda index, d: e_all.at[index])
    ry, rz = nz * cap, ny * cap
    a_src[...] = jnp.concatenate([matmul(one, embedded) for one in spreads], axis=1).astype(BF16)

    def first_leg(group, src, mid):
        done = exchange("y", group, part_of(src, ry), part_of(mid, ry))
        mid[pl.ds(pl.multiple_of(y * ry, ry), ry), :] = src[pl.ds(pl.multiple_of(y * ry, ry), ry), :]
        return done

    def second_leg(group, mid, turned_ref, final):
        turned_ref[...] = matmul(perm_ref[...], mid[...]).astype(BF16)
        done = exchange("z", group, part_of(turned_ref, rz), part_of(final, rz))
        final[pl.ds(pl.multiple_of(z * rz, rz), rz), :] = turned_ref[pl.ds(pl.multiple_of(z * rz, rz), rz), :]
        return done

    a_first = first_leg(1, a_src, a_y)
    lax.fori_loop(cut[2], cut[3], table_step, 0)

    score_scale = math.log2(math.e) / math.sqrt(HD)
    mask_rows = (normalize(mask + tile_pos[...]) * dec_gain).astype(BF16)
    mask_query = contract_last(mask_rows, wq_ref[...]) * score_scale

    e_done()
    full = jnp.concatenate([e_all[i] for i in range(nx)], axis=1).astype(F32)
    vis_rows = (normalize(full + vis_pos) * dec_gain).astype(BF16)
    joint = contract_last(vis_rows, jnp.concatenate([wv_ref[...], wk_ref[...], wq_ref[...]], axis=0))
    query = (joint[:, kv_cols:] * score_scale).astype(BF16)
    q_src[...] = jnp.concatenate([matmul(one, query) for one in spreads], axis=1).astype(BF16)
    q_first = first_leg(2, q_src, q_y)
    vis_kv = joint[:, :kv_cols].astype(BF16)
    for i in range(images):
        kv[i, :vis, :] = vis_kv[i * vis : (i + 1) * vis]
    axes = [("y", "z"), ("z", "y")]
    firsts, seconds = [], [[] for _ in range(images)]

    def slots(i, first, last, outer=0):
        lead = outer * sizes[axes[i][0]]
        return kv.at[i, (lead + first) * vis : (lead + last) * vis]

    def place_of(axis, d):
        return near_first(sizes[axis]).index(d)

    for i in range(images):
        one, two = axes[i]
        firsts.append(
            exchange(
                one,
                3,
                lambda index, i=i: slots(i, 0, 1),
                lambda index, d, i=i, one=one: slots(i, place_of(one, d), place_of(one, d) + 1),
            )
        )

    def forward(i, group, first, last, steps=None):
        two = axes[i][1]
        seconds[i].append(
            exchange(
                two,
                group,
                lambda index: slots(i, first, last),
                lambda index, d: slots(i, first, last, place_of(two, d)),
                steps,
            )
        )

    def relay(i, group, first, last, carried):
        two = axes[i][1]
        send, recv = sems[two]
        copies = {}
        for second in carried:
            second([2, 6])
        for total, via in ((4, 2), (3, 2), (5, 6)):
            copies[total] = pltpu.make_async_remote_copy(
                src_ref=slots(i, first, last, place_of(two, via)),
                dst_ref=slots(i, first, last, place_of(two, total)),
                send_sem=send.at[group, total - 1],
                recv_sem=recv.at[group, total - 1],
                device_id=partner(two, (total - via) % sizes[two])[1],
                device_id_type=MESH,
            )
            copies[total].start()
            pending.append(copies[total])

        def arrived(wanted):
            for d in [d for d in wanted if d in copies]:
                back = partner(two, sizes[two] - d)[1]
                pltpu.make_async_remote_copy(
                    src_ref=slots(i, first, last, place_of(two, d)),
                    dst_ref=slots(i, first, last, place_of(two, d)),
                    send_sem=send.at[group, d - 1],
                    recv_sem=recv.at[group, d - 1],
                    device_id=back,
                    device_id_type=MESH,
                ).wait_recv()
                del copies[d]

        return arrived

    relayed = ny == 8 and nz == 8
    close = [1, 7, 2, 6] if relayed else None
    relays = [[] for _ in range(images)]

    def cuts(size):
        return [(1, 3), (3, 5), (5, 8)] if size == 8 else [(1, size)]

    a_first()
    a_second = second_leg(1, a_y, a_mid, a_z)
    for i in range(images):
        forward(i, 4, 0, 1, close)
    for number in range(len(cuts(ny))):
        for i in range(images)[::-1]:
            if number == 0 and i == 0:
                q_first()
                q_second = second_leg(2, q_y, q_mid, q_z)
            size = sizes[axes[i][0]]
            first, last = cuts(size)[number]
            firsts[i](near_first(size)[first:last])
            forward(i, 5 + number, first, last, close if number < 2 else None)
    a_second()
    res_done = exchange("x", 3, part_of(a_z, own_rows), lambda index, d: res_recv.at[index])
    res_recv[mx] = a_z[pl.ds(pl.multiple_of(mx * own_rows, own_rows), own_rows), :]

    flags_z()
    bias_row, bias_from = iota((ny * 16, 16), 0), iota((ny * 16, 16), 1)
    unpack = jnp.where(
        (bias_row % 16 < images) & (bias_from == (bias_row // 16) * images + bias_row % 16), 1.0, 0.0
    ).astype(BF16)
    for zs in range(nz):
        part = matmul(unpack, f_z[zs]).astype(BF16)
        for ys in range(ny):
            kb[:, (zs * ny + ys) * TILE : (zs * ny + ys + 1) * TILE] = part[ys * 16 : (ys + 1) * 16]
    every_flag = jnp.concatenate([f_z[zs] for zs in range(nz)], axis=0)
    slot_row, slot_from = iota((TILE, nz * 16), 0), iota((TILE, nz * 16), 1)
    source_row = slot_row // cap
    here_lane = iota((TILE, TILE), 1) == seq * cap + iota((TILE, TILE), 0) % cap
    presents = []
    for i in range(images):
        choose = jnp.where(slot_from == (source_row // ny) * 16 + (source_row % ny) * images + i, 1.0, 0.0)
        seen = jnp.where(here_lane, matmul(choose.astype(BF16), every_flag), 0.0)
        presents.append(jnp.where(jnp.sum(seen, axis=1, keepdims=True) < -1.0, 1.0, 0.0))
    if relayed:
        for i in range(images)[::-1]:
            relays[i].append(relay(i, 8, 0, 3, seconds[i][:2]))
    taken_ref[...] = jnp.concatenate([jnp.broadcast_to(one, (TILE, TILE)) for one in presents], axis=1)
    q_second()
    lane = iota((TILE, cols), 1)
    head_masks = [jnp.where(lane // HD == h, 1.0, 0.0) for h in range(cols // HD)]
    heads = len(head_masks)
    found_q = q_z[...]
    block = math.gcd(2048, tiles * TILE)
    lookups = []
    stacked = []
    for i in range(images):
        here = jnp.where(presents[i] > 0, found_q[:, i * cols : (i + 1) * cols].astype(F32), mask_query)
        stacked.append(jnp.concatenate([here * one for one in head_masks], axis=0).astype(BF16))

    def fold(state, scores, values_of):
        top, total, accum = state
        new_top = jnp.maximum(top, jnp.max(scores, axis=1, keepdims=True))
        fix = jnp.exp2(top - new_top)
        expo = jnp.exp2(scores - new_top)
        total = total * fix + jnp.sum(expo, axis=1, keepdims=True)
        accum = accum * fix + values_of(expo.astype(BF16))
        return new_top, total, accum

    for i in range(images):
        select = jnp.where(iota((heads * TILE, 16), 1) == i, 1.0, 0.0).astype(BF16)
        lookups.append(jnp.concatenate([stacked[i], select], axis=1))

    def masked_block(number, states):
        where = slice(number * block, (number + 1) * block)
        keys = jnp.concatenate([kt[:, where], kb[:, where]], axis=0)
        scores = [matmul(one, keys) for one in lookups]
        return tuple(
            fold(state, one, lambda expo: contract_last(expo, vt[:, where])) for state, one in zip(states, scores)
        )

    start = (
        jnp.full((heads * TILE, 1), BIG, F32),
        jnp.zeros((heads * TILE, 1), F32),
        jnp.zeros((heads * TILE, cols), F32),
    )
    states = (start,) * images
    for number in range(tiles * TILE // block):
        states = masked_block(number, states)
        if relayed and number == 0:
            for i in range(images)[::-1]:
                relays[i].append(relay(i, 9, 3, 5, seconds[i][2:3]))

    lookups = [jnp.concatenate([jnp.zeros_like(one), one], axis=1) for one in stacked]

    def visible(states, first, last):
        spans = [slice(first * sizes[axes[i][0]] * vis, last * sizes[axes[i][0]] * vis) for i in range(images)]
        scores = [contract_last(lookups[i], kv[i, spans[i], :]) for i in range(images)]
        return [
            fold(states[i], scores[i], lambda expo, i=i: matmul(expo, kv[i, spans[i], :])[:, :cols])
            for i in range(images)
        ]

    near = 5 if nz == 8 else 1
    for first, last in ((0, near), (near, nz)):
        for i in range(images):
            for second in seconds[i] + relays[i]:
                second(near_first(sizes[axes[i][1]])[max(first, 1) : last])
        states = visible(states, first, last)
    gathered = []
    for i in range(images):
        top, total, accum = states[i]
        accum = accum / total
        attended = jnp.zeros((TILE, cols), F32)
        for h in range(heads):
            attended = attended + accum[h * TILE : (h + 1) * TILE] * head_masks[h]
        gathered.append(attended)
    att_send[...] = jnp.concatenate(gathered, axis=1).astype(BF16)
    sent = len(pending)
    att_done = exchange("x", 5, part_of(att_send, own_rows), lambda index, d: att_recv.at[index])
    tile_mine = pl.ds(pl.multiple_of(mx * own_rows, own_rows), own_rows)
    att_recv[mx] = att_send[tile_mine, :]

    res_done()
    my_pos = tile_pos[tile_mine, :]
    chunk = width // nx
    bases = []
    for i in range(images):
        rows_here = jnp.concatenate(
            [res_recv[j, :, i * chunk : (i + 1) * chunk] for j in range(nx)], axis=1
        ).astype(F32)
        present = taken_ref[tile_mine, i * TILE : i * TILE + 1]
        bases.append(jnp.where(present > 0, rows_here, mask) + my_pos)
    for copy in pending[:sent]:
        copy.wait_send()
    wp_done()
    att_done()
    sums = jnp.concatenate(bases, axis=0)
    for j in range(nx):
        pieces = [att_recv[j, :, i * cols : (i + 1) * cols] for i in range(images)]
        sums = sums + matmul(jnp.concatenate(pieces, axis=0), wp_all[j])
    for i in range(images):
        out_ref[i] = sums[i * own_rows : (i + 1) * own_rows].astype(BF16)
    for copy in pending[sent:]:
        copy.wait_send()


def local(
    enc_tokens,
    enc_gain,
    enc_bias,
    w_in,
    w_out,
    final_gain,
    w_embed,
    dest,
    mask_token,
    dec_gain,
    w_query,
    w_key,
    w_value,
    w_proj,
):
    images, vis, model_width = enc_tokens.shape
    seq_count = lax.axis_size("seq")
    nx = lax.axis_size("mp")
    ny = math.isqrt(seq_count)
    nz = seq_count // ny
    width = mask_token.shape[0]
    cols = w_query.shape[1]
    cap = TILE // seq_count
    rows = images * vis
    own = TILE // nx
    patches = seq_count * TILE

    low = min(4, seq_count // 2)
    s_low, t, c = np.meshgrid(np.arange(low), np.arange(seq_count), np.arange(cap), indexing="ij")
    place = (s_low * cap + t * TILE + c).reshape(-1)
    wave_t = waves(int(place.max()) + 1, 1, width)[place].T.astype(jnp.bfloat16)
    near = waves(TILE, 1, width)
    far = waves(seq_count, TILE, width)
    rot = waves(seq_count // low, low * cap, width)
    zi, yi, ci = np.meshgrid(np.arange(nz), np.arange(ny), np.arange(cap), indexing="ij")
    perm = np.zeros((TILE, TILE), np.float32)
    perm[np.arange(TILE), ((yi * nz + zi) * cap + ci).reshape(-1)] = 1.0

    hbm = pl.BlockSpec(memory_space=pltpu.HBM)
    vmem = pl.BlockSpec(memory_space=pltpu.VMEM)
    operands = (
        enc_tokens.reshape(rows, model_width),
        enc_gain,
        enc_bias,
        w_in,
        w_out,
        w_proj,
        dest.transpose(0, 2, 1),
        jnp.asarray(far),
        jnp.asarray(near),
        mask_token,
        dec_gain,
        w_key.T,
        w_value.T,
        jnp.asarray(wave_t),
        jnp.asarray(rot),
        final_gain,
        w_embed,
        jnp.asarray(perm, BF16),
        w_query.T,
    )
    block_rows = rows // nx
    dma = pltpu.SemaphoreType.DMA
    scratch = [
        *[pltpu.VMEM(operand.shape, operand.dtype) for operand in operands],
        pltpu.VMEM((rows, model_width), F32),
        pltpu.VMEM((rows, model_width), BF16),
        pltpu.VMEM((nx - 1, block_rows, model_width), BF16),
        pltpu.VMEM((rows, model_width), BF16),
        pltpu.VMEM((nx, rows, width // nx), BF16),
        *[pltpu.VMEM((TILE, images * width // nx), BF16)] * 4,
        *[pltpu.VMEM((TILE, images * cols), BF16)] * 4,
        pltpu.VMEM((images, seq_count * vis, 2 * cols), BF16),
        pltpu.VMEM((cols, patches), BF16),
        pltpu.VMEM((16, patches), BF16),
        pltpu.VMEM((cols, patches), BF16),
        pltpu.VMEM((nx, own, images * width // nx), BF16),
        pltpu.VMEM((TILE, width), F32),
        pltpu.VMEM((2 * cols + 16, width), F32),
        pltpu.VMEM((ny, 16, TILE), BF16),
        pltpu.VMEM((nz, 16, TILE), BF16),
        pltpu.VMEM((TILE, images * TILE), F32),
        pltpu.VMEM((nx, cols, width), BF16),
        pltpu.VMEM((TILE, images * cols), BF16),
        pltpu.VMEM((nx, own, images * cols), BF16),
        dma((len(operands),)),
        dma((6, nx - 1)),
        dma((6, nx - 1)),
        dma((10, ny - 1)),
        dma((10, ny - 1)),
        dma((10, nz - 1)),
        dma((10, nz - 1)),
    ]
    return pl.pallas_call(
        functools.partial(kernel, (nx, ny, nz, images, vis)),
        out_shape=pltpu.VMEM((images, own, width), BF16),
        in_specs=[hbm] * len(operands),
        out_specs=vmem,
        scratch_shapes=scratch,
        compiler_params=pltpu.CompilerParams(
            collective_id=0, has_side_effects=True, vmem_limit_bytes=63300000
        ),
    )(*operands)


def solution(mesh):
    placed = (
        P("dp", "seq", None),
        P(),
        P(),
        P(None, "mp"),
        P("mp", None),
        P(),
        P(None, "mp"),
        P("dp", "seq", None),
        P(),
        P(),
        P(None, "mp"),
        P(None, "mp"),
        P(None, "mp"),
        P("mp", None),
    )
    return jax.shard_map(
        local, mesh=mesh, in_specs=placed, out_specs=P("dp", ("seq", "mp"), None), check_vma=False
    )
```
